512 devices in a mesh: dp: 64 (over z, y), tensor: 8 (over x, core).
Axes of the slice: x: 4, y: 4, z: 16, core: 2. Of those that a mesh axis runs over, the one named last changes fastest.
Arguments:
- query_rows: bfloat16 [24576, 3072], P('dp', 'tensor'), may hold values from -60 to 60
- key_rows: bfloat16 [24576, 3072], P('dp', 'tensor'), may hold values from -60 to 60
- value_rows: bfloat16 [24576, 3072], P('dp', 'tensor'), may hold values from -6 to 6
- kept_mask: int32 [24576], P('dp'), may hold values from 0 to 1, as said below
- block_dest: int32 [4096], P('dp'), may hold values from 0 to 63, as said below
- pack_offset: int32 [4096], P('dp'), may hold values from 0 to 319, as said below
- pack_image: int32 [20480], P('dp'), may hold values from 0 to 3, as said below
- grad_attended: bfloat16 [20480, 3072], P('dp', 'tensor'), may hold values from -18 to 18
Outputs:
- attended: bfloat16 [20480, 3072], P('dp', 'tensor')
- query_grad: bfloat16 [24576, 3072], P('dp', 'tensor')
- key_grad: bfloat16 [24576, 3072], P('dp', 'tensor')
- value_grad: bfloat16 [24576, 3072], P('dp', 'tensor')
The draws below stay inside these ranges and needn't reach their ends.
Inputs may be any that keep to these rules, and one draw needn't show every extreme that they name: `kept_mask`: every block of 6 slots keeps at least one slot. `block_dest`: the 64 blocks of one data shard go to 64 different packs. `pack_offset`: in each pack the runs that start at these rows, with the kept counts of the blocks sent there as lengths, tile the 320 rows exactly. `pack_image`: every pack holds exactly 4 images, each one run of rows, numbered in order from 0.
All inputs are finite; a program needn't handle non-finite values.
Results may differ from the reference program's by a relative error of at most 0.0098.
Values may be sent and summed in bfloat16 or wider, within the bound.
A program may use at most 64 MiB of HBM per device.

```python
import math
import jax
import jax.numpy as jnp
from jax import lax

HDIM = 128
HEADS = 24
PACK = 320
SHARDS = 64
SLOTS = 384
BLOCK = 6
IMAGES = 4
WIDTH = 3072
ROWS_SRC = 24576
ROWS_PACK = 20480


def route_plan(key):
    base = jax.random.fold_in(key, 101)
    keys = jax.random.split(base, 6)
    levels = jax.random.randint(keys[0], (SHARDS,), 0, 3)
    whole_source = jax.random.randint(keys[1], (SHARDS,), 0, SHARDS)
    shuffles = jax.vmap(lambda sub: jax.random.permutation(sub, SLOTS))(jax.random.split(keys[2], SHARDS)).astype(jnp.int32)
    units = jnp.arange(SLOTS, dtype=jnp.int32)
    unit_source = units // BLOCK
    unit_row = units % BLOCK
    scores = shuffles + SLOTS * levels[unit_source][None, :]
    scores = scores + 4 * SLOTS * (unit_source[None, :] == whole_source[:, None]).astype(jnp.int32)
    scores = scores + 8 * SLOTS * (unit_row == 0).astype(jnp.int32)[None, :]
    order = jnp.argsort(scores, axis=1, stable=True)
    ranks = jnp.argsort(order, axis=1, stable=True)
    dropped = (ranks < SLOTS - PACK).astype(jnp.int32)
    counts = BLOCK - jnp.sum(dropped.reshape(SHARDS, SHARDS, BLOCK), axis=2)
    dests = jax.vmap(lambda sub: jax.random.permutation(sub, SHARDS))(jax.random.split(keys[3], SHARDS)).astype(jnp.int32)
    source_line = jnp.arange(SHARDS, dtype=jnp.int32)
    block_counts = counts[dests, source_line[:, None]]
    positions = jax.vmap(lambda sub: jax.random.permutation(sub, BLOCK))(jax.random.split(keys[4], SHARDS * SHARDS))
    positions = positions.reshape(SHARDS, SHARDS, BLOCK).astype(jnp.int32)
    kept = (positions < block_counts[:, :, None]).astype(jnp.int32)
    orders = jax.vmap(lambda sub: jax.random.permutation(sub, SHARDS))(jax.random.split(keys[5], SHARDS)).astype(jnp.int32)
    earlier = orders[:, None, :] < orders[:, :, None]
    offsets = jnp.sum(jnp.where(earlier, counts[:, None, :], 0), axis=2)
    return (kept.reshape(-1).astype(jnp.int32), dests.reshape(-1).astype(jnp.int32), offsets.reshape(-1).astype(jnp.int32))


def feature_field(key, row_span):
    keys = jax.random.split(key, 3)
    columns = jnp.arange(WIDTH, dtype=jnp.float32) / WIDTH
    column_scale = jnp.exp(math.log(10.0) * (columns - 0.5) + jax.random.uniform(keys[1], (WIDTH,), minval=-0.4, maxval=0.4))
    row_scale = jnp.exp(jax.random.uniform(keys[2], (ROWS_SRC, 1), minval=-0.5, maxval=0.5) * math.log(row_span))
    gaussian = jnp.clip(jax.random.normal(keys[0], (ROWS_SRC, WIDTH)), -4.0, 4.0)
    base = gaussian
    return jnp.clip(base * column_scale[None, :] * row_scale, -60.0, 60.0)


def draw_query_rows(key, part):
    key = jax.random.fold_in(key, 11)
    return feature_field(key, 10.0).astype(jnp.bfloat16)


def draw_key_rows(key, part):
    key = jax.random.fold_in(key, 12)
    return feature_field(key, 10.0).astype(jnp.bfloat16)


def draw_kept_mask(key, part):
    shared = route_plan(key)
    return shared[0]


def draw_block_dest(key, part):
    shared = route_plan(key)
    return shared[1]


def draw_pack_offset(key, part):
    shared = route_plan(key)
    return shared[2]


def draw_pack_image(key, part):
    key = jax.random.fold_in(key, 4)
    line = jnp.arange(PACK, dtype=jnp.int32)

    def one_pack(sub):
        cuts = jax.random.permutation(sub, PACK - 1)[:IMAGES - 1].astype(jnp.int32) + 1
        return jnp.sum((cuts[None, :] <= line[:, None]).astype(jnp.int32), axis=1)
    return jax.vmap(one_pack)(jax.random.split(key, SHARDS)).reshape(-1).astype(jnp.int32)


def steps_of(stream_key, shape, shards, smallest, high):
    def one(axis_at, blocks):
        heights = jax.random.uniform(jax.random.fold_in(jax.random.fold_in(stream_key, 6), axis_at), (blocks,), jnp.float32, smallest / len(shards), high / len(shards))
        return jnp.repeat(jnp.exp(heights), shape[axis_at] // blocks).reshape((-1,) + (1,) * (len(shape) - axis_at - 1))

    factor_of = one(*shards[0])
    for cut in shards[1:]:
        factor_of = factor_of * one(*cut)
    return factor_of


def scatter_about(key, dims, spread, reach, pieces=(), kind=jnp.bfloat16):
    loudness = steps_of(key, dims, pieces, -0.22, 0.18) if pieces else 1.0
    array = jax.random.normal(key, dims, jnp.float32) * spread * loudness
    return jnp.minimum(jnp.maximum(array, -reach), reach).astype(kind)


def setup_inputs(seed: int = 0) -> dict:
    streams_of = jax.random.split(jax.random.key(seed), 9)
    return {
        "query_rows": draw_query_rows(jax.random.fold_in(streams_of[8], 71), 0),
        "key_rows": draw_key_rows(jax.random.fold_in(streams_of[8], 71), 0),
        "value_rows": scatter_about(streams_of[2], (ROWS_SRC, WIDTH), 1.0, 6.0, ((0, 64), (1, 8))),
        "kept_mask": draw_kept_mask(jax.random.fold_in(streams_of[8], 71), 0),
        "block_dest": draw_block_dest(jax.random.fold_in(streams_of[8], 71), 0),
        "pack_offset": draw_pack_offset(jax.random.fold_in(streams_of[8], 71), 0),
        "pack_image": draw_pack_image(jax.random.fold_in(streams_of[8], 71), 0),
        "grad_attended": scatter_about(streams_of[7], (ROWS_PACK, WIDTH), 3.0, 18.0, ((0, 64), (1, 8))),
    }


SOFT_LIMIT = 20.0
EPSILON = 1e-06

def attend_pack(operands):
    packed_query, packed_key, packed_value, cotangent, images = operands
    query_float = packed_query.astype(jnp.float32)
    key_float = packed_key.astype(jnp.float32)
    scale_query = 1.0 / jnp.sqrt(lax.optimization_barrier(jnp.mean(query_float * query_float, axis=1)) + EPSILON)
    scale_key = 1.0 / jnp.sqrt(lax.optimization_barrier(jnp.mean(key_float * key_float, axis=1)) + EPSILON)
    normed_query = query_float * scale_query[:, None]
    normed_key = key_float * scale_key[:, None]
    round_query = normed_query.astype(jnp.bfloat16).astype(jnp.float32).reshape(PACK, HEADS, HDIM)
    round_key = normed_key.astype(jnp.bfloat16).astype(jnp.float32).reshape(PACK, HEADS, HDIM)
    value_heads = packed_value.astype(jnp.float32).reshape(PACK, HEADS, HDIM)
    grad_heads = cotangent.astype(jnp.float32).reshape(PACK, HEADS, HDIM)
    raw_scores = jnp.einsum('qhd,khd->hqk', round_query, round_key) / math.sqrt(HDIM)
    capped = SOFT_LIMIT * jnp.tanh(raw_scores / SOFT_LIMIT)
    same_image = (images[:, None] == images[None, :]).astype(jnp.float32)
    weight = jnp.exp(capped) * same_image[None]
    probs = weight / lax.optimization_barrier(jnp.sum(weight, axis=2, keepdims=True))
    round_probs = probs.astype(jnp.bfloat16).astype(jnp.float32)
    attended = jnp.einsum('hqk,khd->qhd', round_probs, value_heads).astype(jnp.bfloat16).reshape(PACK, WIDTH)
    value_back = jnp.einsum('hqk,qhd->khd', round_probs, grad_heads).astype(jnp.bfloat16).reshape(PACK, WIDTH)
    prob_grad = jnp.einsum('qhd,khd->hqk', grad_heads, value_heads)
    score_grad = probs * (prob_grad - lax.optimization_barrier(jnp.sum(probs * prob_grad, axis=2, keepdims=True))) * (1.0 - (capped / SOFT_LIMIT) ** 2) / math.sqrt(HDIM)
    round_grad = score_grad.astype(jnp.bfloat16).astype(jnp.float32)
    normed_query_grad = jnp.einsum('hqk,khd->qhd', round_grad, round_key).reshape(PACK, WIDTH)
    normed_key_grad = jnp.einsum('hqk,qhd->khd', round_grad, round_query).reshape(PACK, WIDTH)
    query_inner = lax.optimization_barrier(jnp.mean(normed_query_grad * normed_query, axis=1))
    key_inner = lax.optimization_barrier(jnp.mean(normed_key_grad * normed_key, axis=1))
    query_back = (scale_query[:, None] * (normed_query_grad - normed_query * query_inner[:, None])).astype(jnp.bfloat16)
    key_back = (scale_key[:, None] * (normed_key_grad - normed_key * key_inner[:, None])).astype(jnp.bfloat16)
    return (attended, query_back, key_back, value_back)

def reference(query_rows, key_rows, value_rows, kept_mask, block_dest, pack_offset, pack_image, grad_attended):
    blocks = kept_mask.reshape(SHARDS, SHARDS, BLOCK)
    before = jnp.cumsum(blocks, axis=2) - blocks
    dests = block_dest.reshape(SHARDS, SHARDS)
    offsets = pack_offset.reshape(SHARDS, SHARDS)
    sources = jnp.broadcast_to(jnp.arange(SHARDS, dtype=jnp.int32)[:, None], (SHARDS, SHARDS))
    starts = offsets[dests, sources]
    target = (dests[:, :, None] * PACK + starts[:, :, None] + before).reshape(-1).astype(jnp.int32)
    kept = kept_mask == 1
    slot_line = jnp.arange(ROWS_SRC, dtype=jnp.int32)
    spots = jnp.where(kept, target, ROWS_PACK).astype(jnp.int32)
    anchor = jnp.zeros((ROWS_PACK,), jnp.int32).at[spots].set(slot_line, mode='drop')
    packed_query = jnp.take(query_rows, anchor, axis=0).reshape(SHARDS, PACK, WIDTH)
    packed_key = jnp.take(key_rows, anchor, axis=0).reshape(SHARDS, PACK, WIDTH)
    packed_value = jnp.take(value_rows, anchor, axis=0).reshape(SHARDS, PACK, WIDTH)
    cotangent = grad_attended.reshape(SHARDS, PACK, WIDTH)
    images = pack_image.reshape(SHARDS, PACK)
    results = lax.map(attend_pack, (packed_query, packed_key, packed_value, cotangent, images))
    attended = results[0].reshape(ROWS_PACK, WIDTH)
    home = jnp.minimum(target, ROWS_PACK - 1).astype(jnp.int32)

    def unpack(grads):
        flat = grads.reshape(ROWS_PACK, WIDTH)
        return jnp.where(kept[:, None], jnp.take(flat, home, axis=0), jnp.zeros((), flat.dtype))
    return (attended, unpack(results[1]), unpack(results[2]), unpack(results[3]))
```

```python
import math

import jax
import jax.numpy as jnp
from jax import lax
from jax.experimental import pallas as pl
from jax.experimental.pallas import tpu as pltpu
from jax.sharding import PartitionSpec as P

HDIM = 128
WIDTH = 3072
SOFT_LIMIT = 20.0
EPSILON = 1e-06

MESH = pl.DeviceIdType.MESH
BF = jnp.bfloat16
F32 = jnp.float32
I32 = jnp.int32

NZ = 16
NY = 4
SHARDS = NZ * NY
BLOCK = 6
SLOTS = SHARDS * BLOCK
PACK = 320
COLS = 384
HEADS = COLS // HDIM
LANES = 384
TENSOR = 8

Q, K, V, DV, DQ, DK = range(6)


def mm(a, b):
    return lax.dot_general(a, b, (((1,), (0,)), ((), ())), preferred_element_type=F32)


def mm_nt(a, b):
    return lax.dot_general(a, b, (((1,), (1,)), ((), ())), preferred_element_type=F32)


def mm_tn(a, b):
    return lax.dot_general(a, b, (((0,), (0,)), ((), ())), preferred_element_type=F32)


def iota(shape, dim):
    return lax.broadcasted_iota(I32, shape, dim)


def sixth(x):
    return (x * 10923) >> 16


def one_hot(row, rows):
    return jnp.where(iota((rows, row.shape[1]), 0) == row, 1.0, 0.0).astype(BF)


def row_sums(product):
    high = product.astype(BF)
    low = (product - high.astype(F32)).astype(BF)
    ones = jnp.ones((8, COLS), BF)
    return mm_nt(ones, high) + mm_nt(ones, low)


def column(row):
    return jnp.transpose(jnp.broadcast_to(row, (128, LANES)))[:PACK, 0:1]


def kernel(
    kept_ref, dest_ref, offset_ref, image_ref, q_hbm, k_hbm, v_hbm, g_hbm,
    att_ref, dq_ref, dk_ref, dv_ref,
    qkv, cot, ysend, yrecv, zsend, zrecv, xsend, xrecv,
    gather_y, unpack, place, place_y, back_y, regroup, regroup_inv,
    probs, tanhs, packed_q, packed_k, normed_q, normed_k, grad_q, grad_k,
    load_sem, ysend_sem, yrecv_sem, zsend_sem, zrecv_sem, xsend_sem, xrecv_sem,
):
    dp = lax.axis_index("dp")
    tensor = lax.axis_index("tensor")
    z, y = dp // NY, dp % NY

    def y_peer(i):
        return lax.rem(y + i + 1, NY)

    def z_peer(i):
        half = (i + 1) // 2 + (i + 1) % 2
        return lax.rem(z + jnp.where(i % 2 == 0, half, NZ - half), NZ)

    def x_peer(i):
        return lax.rem(tensor + i + 1, TENSOR)

    barrier = pltpu.get_barrier_semaphore()

    def greet_z(i, carry):
        pl.semaphore_signal(
            barrier, inc=1, device_id={"dp": z_peer(i) * NY + y}, device_id_type=MESH
        )
        return carry

    def greet_y(i, carry):
        pl.semaphore_signal(
            barrier, inc=1, device_id={"dp": z * NY + y_peer(i)}, device_id_type=MESH
        )
        return carry

    def greet_x(i, carry):
        pl.semaphore_signal(barrier, inc=1, device_id={"tensor": x_peer(i)}, device_id_type=MESH)
        return carry

    lax.fori_loop(0, NZ - 1, greet_z, 0)
    lax.fori_loop(0, NY - 1, greet_y, 0)
    lax.fori_loop(0, TENSOR - 1, greet_x, 0)

    loads = [
        pltpu.make_async_copy(source, target, load_sem.at[i])
        for i, (source, target) in enumerate(
            ((q_hbm, qkv.at[0]), (k_hbm, qkv.at[1]), (v_hbm, qkv.at[2]), (g_hbm, cot))
        )
    ]
    for load in loads:
        load.start()

    def send_y(array):
        def one(i, carry):
            peer = y_peer(i)
            pltpu.make_async_remote_copy(
                ysend.at[array, peer], yrecv.at[array, y], ysend_sem.at[array], yrecv_sem.at[array],
                device_id={"dp": z * NY + peer}, device_id_type=MESH,
            ).start()
            return carry

        lax.fori_loop(0, NY - 1, one, 0)
        yrecv[array, y] = ysend[array, y]

    def wait_y(array):
        part = yrecv.at[array, pl.ds(0, NY - 1)]
        pltpu.make_async_copy(part, part, yrecv_sem.at[array]).wait()
        return yrecv[array].reshape(SLOTS, COLS)

    def send_z(array):
        def one(i, carry):
            peer = z_peer(i)
            pltpu.make_async_remote_copy(
                zsend.at[array, peer], zrecv.at[array, z], zsend_sem.at[array], zrecv_sem.at[array],
                device_id={"dp": peer * NY + y}, device_id_type=MESH,
            ).start()
            return carry

        lax.fori_loop(0, NZ - 1, one, 0)
        zrecv[array, z] = zsend[array, z]

    def wait_z(array):
        part = zrecv.at[array, pl.ds(0, NZ - 1)]
        pltpu.make_async_copy(part, part, zrecv_sem.at[array]).wait()
        return zrecv[array].reshape(SLOTS, COLS)

    def send_x(which):
        def one(i, carry):
            peer = x_peer(i)
            pltpu.make_async_remote_copy(
                xsend.at[which], xrecv.at[which, tensor], xsend_sem.at[which], xrecv_sem.at[which],
                device_id={"tensor": peer}, device_id_type=MESH,
            ).start()
            return carry

        lax.fori_loop(0, TENSOR - 1, one, 0)
        xrecv[which, tensor] = xsend[which]

    def wait_x(which):
        part = xrecv.at[which, pl.ds(0, TENSOR - 1)]
        pltpu.make_async_copy(part, part, xrecv_sem.at[which]).wait()
        return jnp.sum(xrecv[which], axis=0)

    def put_y(array, rows):
        ysend[array] = rows.astype(BF).reshape(NY, SLOTS // NY, COLS)

    def put_z(array, rows):
        zsend[array] = rows.astype(BF).reshape(NZ, SLOTS // NZ, COLS)

    line = iota((1, SLOTS), 1)
    unit = sixth(line)
    spot = line - BLOCK * unit
    unit_y = (unit & (NZ - 1)) * NY + (unit >> 4)
    down = iota((SLOTS, SLOTS), 0)
    across = iota((SLOTS, SLOTS), 1)
    earlier = jnp.where((sixth(down) == sixth(across)) & (down < across), 1.0, 0.0).astype(BF)
    kept = kept_ref[...]
    before = mm(jnp.broadcast_to(kept.astype(F32), (8, SLOTS)).astype(BF), earlier)[0:1]
    before = before.astype(I32)
    which = iota((8, SHARDS), 0)
    dest = dest_ref[...]
    offset = offset_ref[...]
    parts = jnp.where(which == 0, dest, jnp.where(which == 1, offset >> 4, offset & 15))
    parts = parts.astype(F32).astype(BF)
    spread = mm(parts, one_hot(unit, SHARDS)).astype(I32)
    spread_y = mm(parts, one_hot(unit_y, SHARDS)).astype(I32)
    dest_slot = spread[0:1]
    first = spread[1:2] * 16 + spread[2:3]
    first_y = spread_y[1:2] * 16 + spread_y[2:3]
    dest_y = (dest_slot & (NY - 1)) * NZ + (dest_slot >> 2)
    target = jnp.where(kept == 1, dest_slot * BLOCK + before, -1)
    target_y = jnp.where(kept == 1, dest_y * BLOCK + before, -1)

    gather = one_hot(target, SLOTS)
    loads[0].wait()
    put_z(Q, mm(gather, qkv[0]))
    pl.semaphore_wait(barrier, (NZ - 1) + (NY - 1) + (TENSOR - 1))
    send_z(Q)

    gather_y[...] = one_hot(target_y, SLOTS)
    loads[1].wait()
    put_y(K, mm(gather_y[...], qkv[1]))
    send_y(K)
    loads[2].wait()
    put_y(V, mm(gather_y[...], qkv[2]))
    send_y(V)

    identity = jnp.where(down == across, 1.0, 0.0).astype(BF)
    regroup[...] = one_hot(unit_y * BLOCK + spot, SLOTS)
    put_z(K, mm(regroup[...], wait_y(K)))
    send_z(K)
    put_z(V, mm(regroup[...], wait_y(V)))
    send_z(V)

    unpack[...] = mm_nt(identity, gather).astype(BF)
    place[...] = one_hot(first + spot, PACK)
    place_y[...] = one_hot(first_y + spot, PACK)
    back_y[...] = mm_nt(identity, place_y[...]).astype(BF)
    unit_n = (unit & (NY - 1)) * NZ + (unit >> 2)
    regroup_inv[...] = one_hot(unit_n * BLOCK + spot, SLOTS)

    image = jnp.broadcast_to(image_ref[...], (8, PACK))
    image_hot = jnp.where(image == iota((8, PACK), 0), 1.0, 0.0).astype(BF)
    same = mm_tn(image_hot, image_hot)

    xsend[...] = jnp.zeros((3, 8, LANES), F32)

    put_y(Q, mm(regroup_inv[...], wait_z(Q)))
    send_y(Q)
    packed = mm(place_y[...], wait_y(Q))
    packed_q[...] = packed
    xsend[0, :, :PACK] = row_sums(packed * packed)
    send_x(0)

    packed = mm(place[...], wait_z(K))
    packed_k[...] = packed
    xsend[1, :, :PACK] = row_sums(packed * packed)
    send_x(1)

    scale_q = column(lax.rsqrt(wait_x(0)[0:1] / WIDTH + EPSILON))
    packed_q[...] = packed_q[...] * scale_q
    normed_q[...] = packed_q[...].astype(BF)
    scale_k = column(lax.rsqrt(wait_x(1)[0:1] / WIDTH + EPSILON))
    packed_k[...] = packed_k[...] * scale_k
    normed_k[...] = packed_k[...].astype(BF)

    loads[3].wait()
    value_back = []
    for h in range(HEADS):
        cols = slice(h * HDIM, (h + 1) * HDIM)
        raw = mm_nt(normed_q[:, cols], normed_k[:, cols]) / math.sqrt(HDIM)
        bent = jnp.tanh(raw / SOFT_LIMIT)
        weight = jnp.exp(SOFT_LIMIT * bent) * same
        prob = weight / jnp.sum(weight, axis=1, keepdims=True)
        probs[h] = prob
        tanhs[h] = bent
        value_back.append(mm_tn(prob.astype(BF), cot[:, cols]).astype(BF))
    put_y(DV, mm(back_y[...], jnp.concatenate(value_back, axis=1)))
    send_y(DV)
    put_z(DV, mm(regroup[...], wait_y(DV)))
    send_z(DV)

    value = mm(place[...], wait_z(V)).astype(BF)
    for h in range(HEADS):
        cols = slice(h * HDIM, (h + 1) * HDIM)
        prob = probs[h]
        bent = tanhs[h]
        prob_grad = mm_nt(cot[:, cols], value[:, cols])
        inner = jnp.sum(prob * prob_grad, axis=1, keepdims=True)
        score = prob * (prob_grad - inner) * (1.0 - bent * bent) / math.sqrt(HDIM)
        score = score.astype(BF)
        grad_q[:, cols] = mm(score, normed_k[:, cols])
        grad_k[:, cols] = mm_tn(score, normed_q[:, cols])
    sums_q = row_sums(grad_q[...] * packed_q[...])
    sums_k = row_sums(grad_k[...] * packed_k[...])
    xsend[2, :, :PACK] = jnp.where(iota((8, PACK), 0) == 0, sums_q, sums_k)
    send_x(2)
    for h in range(HEADS):
        cols = slice(h * HDIM, (h + 1) * HDIM)
        att_ref[:, cols] = mm(probs[h].astype(BF), value[:, cols]).astype(BF)
    inner = wait_x(2) / WIDTH
    back = scale_q * (grad_q[...] - packed_q[...] * column(inner[0:1]))
    put_y(DQ, mm(back_y[...], back.astype(BF)))
    send_y(DQ)
    back = scale_k * (grad_k[...] - packed_k[...] * column(inner[1:2]))
    put_y(DK, mm(back_y[...], back.astype(BF)))
    send_y(DK)
    put_z(DQ, mm(regroup[...], wait_y(DQ)))
    send_z(DQ)
    put_z(DK, mm(regroup[...], wait_y(DK)))
    send_z(DK)

    dv_ref[...] = mm(unpack[...], wait_z(DV)).astype(BF)
    dq_ref[...] = mm(unpack[...], wait_z(DQ)).astype(BF)
    dk_ref[...] = mm(unpack[...], wait_z(DK)).astype(BF)

    for array in range(6):
        part = ysend.at[array, pl.ds(0, NY - 1)]
        pltpu.make_async_copy(part, part, ysend_sem.at[array]).wait()
        part = zsend.at[array, pl.ds(0, NZ - 1)]
        pltpu.make_async_copy(part, part, zsend_sem.at[array]).wait()
    for which in range(3):
        part = xrecv.at[which, pl.ds(0, TENSOR - 1)]
        pltpu.make_async_copy(part, part, xsend_sem.at[which]).wait()


def local(
    query_rows, key_rows, value_rows, kept_mask, block_dest, pack_offset, pack_image, grad_attended
):
    vmem = pl.BlockSpec(memory_space=pltpu.VMEM)
    hbm = pl.BlockSpec(memory_space=pl.ANY)
    dma = pltpu.SemaphoreType.DMA
    slots = jax.ShapeDtypeStruct((SLOTS, COLS), BF)
    square = pltpu.VMEM((SLOTS, SLOTS), BF)
    return pl.pallas_call(
        kernel,
        out_shape=(jax.ShapeDtypeStruct((PACK, COLS), BF), slots, slots, slots),
        in_specs=[vmem] * 4 + [hbm] * 4,
        out_specs=(vmem,) * 4,
        scratch_shapes=[
            pltpu.VMEM((3, SLOTS, COLS), BF),
            pltpu.VMEM((PACK, COLS), BF),
            pltpu.VMEM((6, NY, SLOTS // NY, COLS), BF),
            pltpu.VMEM((6, NY, SLOTS // NY, COLS), BF),
            pltpu.VMEM((6, NZ, SLOTS // NZ, COLS), BF),
            pltpu.VMEM((6, NZ, SLOTS // NZ, COLS), BF),
            pltpu.VMEM((3, 8, LANES), F32),
            pltpu.VMEM((3, TENSOR, 8, LANES), F32),
            square,
            square,
            pltpu.VMEM((PACK, SLOTS), BF),
            pltpu.VMEM((PACK, SLOTS), BF),
            pltpu.VMEM((SLOTS, PACK), BF),
            square,
            square,
            pltpu.VMEM((HEADS, PACK, PACK), F32),
            pltpu.VMEM((HEADS, PACK, PACK), F32),
            pltpu.VMEM((PACK, COLS), F32),
            pltpu.VMEM((PACK, COLS), F32),
            pltpu.VMEM((PACK, COLS), BF),
            pltpu.VMEM((PACK, COLS), BF),
            pltpu.VMEM((PACK, COLS), F32),
            pltpu.VMEM((PACK, COLS), F32),
            dma((4,)),
            dma((6,)),
            dma((6,)),
            dma((6,)),
            dma((6,)),
            dma((3,)),
            dma((3,)),
        ],
        compiler_params=pltpu.CompilerParams(
            collective_id=0, has_side_effects=True, vmem_limit_bytes=48 * 2**20
        ),
        cost_estimate=pl.CostEstimate(
            flops=4 * 10**9, bytes_accessed=3 * 10**6, transcendentals=10**6
        ),
        name="repack_attention",
    )(
        kept_mask.reshape(1, SLOTS),
        block_dest.reshape(1, SHARDS),
        pack_offset.reshape(1, SHARDS),
        pack_image.reshape(1, PACK),
        query_rows,
        key_rows,
        value_rows,
        grad_attended,
    )


def solution(mesh):
    in_specs = (
        P("dp", "tensor"),
        P("dp", "tensor"),
        P("dp", "tensor"),
        P("dp"),
        P("dp"),
        P("dp"),
        P("dp"),
        P("dp", "tensor"),
    )
    out_specs = (P("dp", "tensor"), P("dp", "tensor"), P("dp", "tensor"), P("dp", "tensor"))
    return jax.shard_map(local, mesh=mesh, in_specs=in_specs, out_specs=out_specs, check_vma=False)
```

```python
import math

import jax
import jax.numpy as jnp
from jax import lax
from jax.experimental import pallas as pl
from jax.experimental.pallas import tpu as pltpu
from jax.sharding import PartitionSpec as P

HDIM = 128
WIDTH = 3072
SOFT_LIMIT = 20.0
EPSILON = 1e-06

MESH = pl.DeviceIdType.MESH
BF = jnp.bfloat16
F32 = jnp.float32
I32 = jnp.int32

NZ = 16
NY = 4
SHARDS = NZ * NY
BLOCK = 6
SLOTS = SHARDS * BLOCK
PACK = 320
COLS = 384
HEADS = COLS // HDIM
FIRST = 8
LANES = 384
TENSOR = 8

Q, K, V, DV, DQ, DK = range(6)


def mm(a, b):
    return lax.dot_general(a, b, (((1,), (0,)), ((), ())), preferred_element_type=F32)


def mm_nt(a, b):
    return lax.dot_general(a, b, (((1,), (1,)), ((), ())), preferred_element_type=F32)


def mm_tn(a, b):
    return lax.dot_general(a, b, (((0,), (0,)), ((), ())), preferred_element_type=F32)


def iota(shape, dim):
    return lax.broadcasted_iota(I32, shape, dim)


def sixth(x):
    return (x * 10923) >> 16


def one_hot(row, rows):
    return jnp.where(iota((rows, row.shape[1]), 0) == row, 1.0, 0.0).astype(BF)


def row_sums(product):
    high = product.astype(BF)
    low = (product - high.astype(F32)).astype(BF)
    ones = jnp.ones((8, COLS), BF)
    return mm_nt(ones, high) + mm_nt(ones, low)


def column(row):
    return jnp.transpose(jnp.broadcast_to(row, (128, LANES)))[:PACK, 0:1]


def kernel(
    kept_hbm, dest_hbm, offset_hbm, image_hbm, q_hbm, k_hbm, v_hbm, g_hbm,
    att_hbm, dq_hbm, dk_hbm, dv_hbm,
    kept_ref, dest_ref, offset_ref, image_ref, qkv, cot, attended, home, ysend, yrecv, zsend, zrecv, xsend, xrecv,
    gather_y, unpack, unpack_y, place, place_y, back, back_y, regroup, regroup_inv,
    probs, tanhs, packed_q, packed_k, normed_q, normed_k, grad_q, grad_k,
    load_sem, store_sem, ysend_sem, yrecv_sem, zsend_sem, zrecv_sem, xsend_sem, xrecv_sem,
):
    dp = lax.axis_index("dp")
    tensor = lax.axis_index("tensor")
    z, y = dp // NY, dp % NY

    def y_peer(i):
        return lax.rem(y + i + 1, NY)

    def z_peer(i):
        half = NZ // 2 - (i + 1) // 2
        return lax.rem(z + jnp.where(i % 2 == 0, half, NZ - half), NZ)

    def x_peer(i):
        return lax.rem(tensor + i + 1, TENSOR)

    barrier = pltpu.get_barrier_semaphore()

    def greet_z(i, carry):
        pl.semaphore_signal(
            barrier, inc=1, device_id={"dp": z_peer(i) * NY + y}, device_id_type=MESH
        )
        return carry

    def greet_y(i, carry):
        pl.semaphore_signal(
            barrier, inc=1, device_id={"dp": z * NY + y_peer(i)}, device_id_type=MESH
        )
        return carry

    def greet_x(i, carry):
        pl.semaphore_signal(barrier, inc=1, device_id={"tensor": x_peer(i)}, device_id_type=MESH)
        return carry

    lax.fori_loop(0, NZ - 1, greet_z, 0)
    lax.fori_loop(0, NY - 1, greet_y, 0)
    lax.fori_loop(0, TENSOR - 1, greet_x, 0)

    loads = [
        pltpu.make_async_copy(source, target, load_sem.at[i])
        for i, (source, target) in enumerate(
            (
                (kept_hbm, kept_ref), (dest_hbm, dest_ref), (offset_hbm, offset_ref),
                (image_hbm, image_ref), (q_hbm, qkv.at[0]), (k_hbm, qkv.at[1]),
                (v_hbm, qkv.at[2]), (g_hbm, cot),
            )
        )
    ]
    for load in loads:
        load.start()
    stores = [
        pltpu.make_async_copy(source, target, store_sem.at[i])
        for i, (source, target) in enumerate(
            ((attended, att_hbm), (home.at[0], dv_hbm), (home.at[1], dq_hbm), (home.at[2], dk_hbm))
        )
    ]

    def send_y(array):
        def one(i, carry):
            peer = y_peer(i)
            pltpu.make_async_remote_copy(
                ysend.at[array, peer], yrecv.at[array, y], ysend_sem.at[array], yrecv_sem.at[array],
                device_id={"dp": z * NY + peer}, device_id_type=MESH,
            ).start()
            return carry

        lax.fori_loop(0, NY - 1, one, 0)
        yrecv[array, y] = ysend[array, y]

    def wait_y(array):
        part = yrecv.at[array, pl.ds(0, NY - 1)]
        pltpu.make_async_copy(part, part, yrecv_sem.at[array]).wait()
        return yrecv[array].reshape(SLOTS, COLS)

    def send_z(array):
        def one(i, carry):
            peer = z_peer(i)
            pltpu.make_async_remote_copy(
                zsend.at[array, peer], zrecv.at[array, z],
                zsend_sem.at[array, jnp.where(i < FIRST, 0, 1)], zrecv_sem.at[array],
                device_id={"dp": peer * NY + y}, device_id_type=MESH,
            ).start()
            return carry

        lax.fori_loop(0, NZ - 1, one, 0)
        zrecv[array, z] = zsend[array, z]

    def wait_sent_z(array, half):
        count = FIRST if half == 0 else NZ - 1 - FIRST
        part = zsend.at[array, pl.ds(0, count)]
        pltpu.make_async_copy(part, part, zsend_sem.at[array, half]).wait()

    def wait_z(array):
        part = zrecv.at[array, pl.ds(0, NZ - 1)]
        pltpu.make_async_copy(part, part, zrecv_sem.at[array]).wait()
        return zrecv[array].reshape(SLOTS, COLS)

    def send_x(which):
        def one(i, carry):
            peer = x_peer(i)
            pltpu.make_async_remote_copy(
                xsend.at[which], xrecv.at[which, tensor], xsend_sem.at[which], xrecv_sem.at[which],
                device_id={"tensor": peer}, device_id_type=MESH,
            ).start()
            return carry

        lax.fori_loop(0, TENSOR - 1, one, 0)
        xrecv[which, tensor] = xsend[which]

    def wait_x(which):
        part = xrecv.at[which, pl.ds(0, TENSOR - 1)]
        pltpu.make_async_copy(part, part, xrecv_sem.at[which]).wait()
        return jnp.sum(xrecv[which], axis=0)

    def put_y(array, rows):
        ysend[array] = rows.astype(BF).reshape(NY, SLOTS // NY, COLS)

    def put_z(array, rows):
        zsend[array] = rows.astype(BF).reshape(NZ, SLOTS // NZ, COLS)

    line = iota((1, SLOTS), 1)
    unit = sixth(line)
    spot = line - BLOCK * unit
    unit_y = (unit & (NZ - 1)) * NY + (unit >> 4)
    down = iota((SLOTS, SLOTS), 0)
    across = iota((SLOTS, SLOTS), 1)
    earlier = jnp.where((sixth(down) == sixth(across)) & (down < across), 1.0, 0.0).astype(BF)
    for load in loads[:4]:
        load.wait()
    kept = kept_ref[...].reshape(1, SLOTS)
    before = mm(jnp.broadcast_to(kept.astype(F32), (8, SLOTS)).astype(BF), earlier)[0:1]
    before = before.astype(I32)
    which = iota((8, SHARDS), 0)
    dest = dest_ref[...].reshape(1, SHARDS)
    offset = offset_ref[...].reshape(1, SHARDS)
    parts = jnp.where(which == 0, dest, jnp.where(which == 1, offset >> 4, offset & 15))
    parts = parts.astype(F32).astype(BF)
    spread = mm(parts, one_hot(unit, SHARDS)).astype(I32)
    spread_y = mm(parts, one_hot(unit_y, SHARDS)).astype(I32)
    dest_slot = spread[0:1]
    first = spread[1:2] * 16 + spread[2:3]
    first_y = spread_y[1:2] * 16 + spread_y[2:3]
    dest_y = (dest_slot & (NY - 1)) * NZ + (dest_slot >> 2)
    target = jnp.where(kept == 1, dest_slot * BLOCK + before, -1)
    target_y = jnp.where(kept == 1, dest_y * BLOCK + before, -1)

    gather = one_hot(target, SLOTS)
    loads[4].wait()
    put_z(Q, mm(gather, qkv[0]))
    pl.semaphore_wait(barrier, (NZ - 1) + (NY - 1) + (TENSOR - 1))
    send_z(Q)

    gather_y[...] = one_hot(target_y, SLOTS)
    loads[5].wait()
    put_y(K, mm(gather_y[...], qkv[1]))
    send_y(K)
    loads[6].wait()
    put_y(V, mm(gather_y[...], qkv[2]))
    send_y(V)

    identity = jnp.where(down == across, 1.0, 0.0).astype(BF)
    regroup[...] = one_hot(unit_y * BLOCK + spot, SLOTS)
    unpack[...] = mm_nt(identity, gather).astype(BF)
    place[...] = one_hot(first + spot, PACK)
    place_y[...] = one_hot(first_y + spot, PACK)
    back[...] = mm_nt(identity, place[...]).astype(BF)
    back_y[...] = mm_nt(identity, place_y[...]).astype(BF)
    unpack_y[...] = mm_nt(identity, gather_y[...]).astype(BF)
    unit_n = (unit & (NY - 1)) * NZ + (unit >> 2)
    regroup_inv[...] = one_hot(unit_n * BLOCK + spot, SLOTS)

    image = jnp.broadcast_to(image_ref[...].reshape(1, PACK), (8, PACK))
    image_hot = jnp.where(image == iota((8, PACK), 0), 1.0, 0.0).astype(BF)
    same = mm_tn(image_hot, image_hot)

    xsend[...] = jnp.zeros((3, 8, LANES), F32)

    put_z(K, mm(regroup[...], wait_y(K)))
    put_z(V, mm(regroup[...], wait_y(V)))
    wait_sent_z(Q, 0)
    send_z(K)

    put_y(Q, mm(regroup_inv[...], wait_z(Q)))
    send_y(Q)
    packed = mm(place_y[...], wait_y(Q))
    packed_q[...] = packed
    xsend[0, :, :PACK] = row_sums(packed * packed)
    send_x(0)
    wait_sent_z(K, 0)
    send_z(V)

    packed = mm(place[...], wait_z(K))
    packed_k[...] = packed
    xsend[1, :, :PACK] = row_sums(packed * packed)
    send_x(1)

    scale_q = column(lax.rsqrt(wait_x(0)[0:1] / WIDTH + EPSILON))
    packed_q[...] = packed_q[...] * scale_q
    normed_q[...] = packed_q[...].astype(BF)
    scale_k = column(lax.rsqrt(wait_x(1)[0:1] / WIDTH + EPSILON))
    packed_k[...] = packed_k[...] * scale_k
    normed_k[...] = packed_k[...].astype(BF)

    loads[7].wait()
    value_back = []
    for h in range(HEADS):
        cols = slice(h * HDIM, (h + 1) * HDIM)
        raw = mm_nt(normed_q[:, cols], normed_k[:, cols]) / math.sqrt(HDIM)
        bent = jnp.tanh(raw / SOFT_LIMIT)
        weight = jnp.exp(SOFT_LIMIT * bent) * same
        prob = weight * (1.0 / jnp.sum(weight, axis=1, keepdims=True))
        probs[h] = prob
        tanhs[h] = bent
        value_back.append(mm_tn(prob.astype(BF), cot[:, cols]).astype(BF))
    put_z(DV, mm(back[...], jnp.concatenate(value_back, axis=1)))
    wait_sent_z(V, 0)
    send_z(DV)

    value = mm(place[...], wait_z(V)).astype(BF)
    for h in range(HEADS):
        cols = slice(h * HDIM, (h + 1) * HDIM)
        prob = probs[h]
        bent = tanhs[h]
        prob_grad = mm_nt(cot[:, cols], value[:, cols])
        inner = jnp.sum(prob * prob_grad, axis=1, keepdims=True)
        score = prob * (prob_grad - inner) * (1.0 - bent * bent) / math.sqrt(HDIM)
        score = score.astype(BF)
        grad_q[:, cols] = mm(score, normed_k[:, cols])
        grad_k[:, cols] = mm_tn(score, normed_q[:, cols])
    sums_q = row_sums(grad_q[...] * packed_q[...])
    sums_k = row_sums(grad_k[...] * packed_k[...])
    xsend[2, :, :PACK] = jnp.where(iota((8, PACK), 0) == 0, sums_q, sums_k)
    send_x(2)
    for h in range(HEADS):
        cols = slice(h * HDIM, (h + 1) * HDIM)
        attended[:, cols] = mm(probs[h].astype(BF), value[:, cols]).astype(BF)
    stores[0].start()
    inner = wait_x(2) / WIDTH
    grad = scale_q * (grad_q[...] - packed_q[...] * column(inner[0:1]))
    put_z(DQ, mm(back[...], grad.astype(BF)))
    grad = scale_k * (grad_k[...] - packed_k[...] * column(inner[1:2]))
    put_y(DK, mm(back_y[...], grad.astype(BF)))
    wait_sent_z(DV, 0)
    send_z(DQ)
    send_y(DK)
    put_z(DK, mm(regroup[...], wait_y(DK)))
    put_y(DV, mm(regroup_inv[...], wait_z(DV)))
    send_y(DV)
    wait_sent_z(DQ, 0)
    send_z(DK)
    home[0] = mm(unpack_y[...], wait_y(DV)).astype(BF)
    stores[1].start()
    put_y(DQ, mm(regroup_inv[...], wait_z(DQ)))
    send_y(DQ)
    home[1] = mm(unpack_y[...], wait_y(DQ)).astype(BF)
    stores[2].start()
    home[2] = mm(unpack[...], wait_z(DK)).astype(BF)
    stores[3].start()

    for array in range(6):
        part = ysend.at[array, pl.ds(0, NY - 1)]
        pltpu.make_async_copy(part, part, ysend_sem.at[array]).wait()
        wait_sent_z(array, 1)
    wait_sent_z(DK, 0)
    for which in range(3):
        part = xrecv.at[which, pl.ds(0, TENSOR - 1)]
        pltpu.make_async_copy(part, part, xsend_sem.at[which]).wait()
    for copy in stores:
        copy.wait()


def store(*refs):
    for source, target in zip(refs[:4], refs[4:]):
        target[...] = source[...]


def local(
    query_rows, key_rows, value_rows, kept_mask, block_dest, pack_offset, pack_image, grad_attended
):
    hbm = pl.BlockSpec(memory_space=pltpu.HBM)
    vmem = pl.BlockSpec(memory_space=pltpu.VMEM)
    dma = pltpu.SemaphoreType.DMA
    slots = jax.ShapeDtypeStruct((SLOTS, COLS), BF)
    square = pltpu.VMEM((SLOTS, SLOTS), BF)
    results = pl.pallas_call(
        kernel,
        out_shape=(jax.ShapeDtypeStruct((PACK, COLS), BF), slots, slots, slots),
        in_specs=[hbm] * 8,
        out_specs=(hbm,) * 4,
        scratch_shapes=[
            pltpu.VMEM((SLOTS,), I32),
            pltpu.VMEM((SHARDS,), I32),
            pltpu.VMEM((SHARDS,), I32),
            pltpu.VMEM((PACK,), I32),
            pltpu.VMEM((3, SLOTS, COLS), BF),
            pltpu.VMEM((PACK, COLS), BF),
            pltpu.VMEM((PACK, COLS), BF),
            pltpu.VMEM((3, SLOTS, COLS), BF),
            pltpu.VMEM((6, NY, SLOTS // NY, COLS), BF),
            pltpu.VMEM((6, NY, SLOTS // NY, COLS), BF),
            pltpu.VMEM((6, NZ, SLOTS // NZ, COLS), BF),
            pltpu.VMEM((6, NZ, SLOTS // NZ, COLS), BF),
            pltpu.VMEM((3, 8, LANES), F32),
            pltpu.VMEM((3, TENSOR, 8, LANES), F32),
            square,
            square,
            square,
            pltpu.VMEM((PACK, SLOTS), BF),
            pltpu.VMEM((PACK, SLOTS), BF),
            pltpu.VMEM((SLOTS, PACK), BF),
            pltpu.VMEM((SLOTS, PACK), BF),
            square,
            square,
            pltpu.VMEM((HEADS, PACK, PACK), F32),
            pltpu.VMEM((HEADS, PACK, PACK), F32),
            pltpu.VMEM((PACK, COLS), F32),
            pltpu.VMEM((PACK, COLS), F32),
            pltpu.VMEM((PACK, COLS), BF),
            pltpu.VMEM((PACK, COLS), BF),
            pltpu.VMEM((PACK, COLS), F32),
            pltpu.VMEM((PACK, COLS), F32),
            dma((8,)),
            dma((4,)),
            dma((6,)),
            dma((6,)),
            dma((6, 2)),
            dma((6,)),
            dma((3,)),
            dma((3,)),
        ],
        compiler_params=pltpu.CompilerParams(
            collective_id=0, has_side_effects=True, vmem_limit_bytes=62 * 2**20
        ),
        cost_estimate=pl.CostEstimate(
            flops=4 * 10**9, bytes_accessed=3 * 10**6, transcendentals=10**6
        ),
        name="repack_attention",
    )(
        kept_mask,
        block_dest,
        pack_offset,
        pack_image,
        query_rows,
        key_rows,
        value_rows,
        grad_attended,
    )
    return pl.pallas_call(
        store,
        out_shape=(jax.ShapeDtypeStruct((PACK, COLS), BF), slots, slots, slots),
        in_specs=[vmem] * 4,
        out_specs=(vmem,) * 4,
        compiler_params=pltpu.CompilerParams(vmem_limit_bytes=62 * 2**20),
        name="store_outputs",
    )(*results)


def solution(mesh):
    in_specs = (
        P("dp", "tensor"),
        P("dp", "tensor"),
        P("dp", "tensor"),
        P("dp"),
        P("dp"),
        P("dp"),
        P("dp"),
        P("dp", "tensor"),
    )
    out_specs = (P("dp", "tensor"), P("dp", "tensor"), P("dp", "tensor"), P("dp", "tensor"))
    return jax.shard_map(local, mesh=mesh, in_specs=in_specs, out_specs=out_specs, check_vma=False)
```

```python
import math

import jax
import jax.numpy as jnp
from jax import lax
from jax.experimental import pallas as pl
from jax.experimental.pallas import tpu as pltpu
from jax.sharding import PartitionSpec as P

HDIM = 128
WIDTH = 3072
SOFT_LIMIT = 20.0
EPSILON = 1e-06

MESH = pl.DeviceIdType.MESH
BF = jnp.bfloat16
F32 = jnp.float32
I32 = jnp.int32

NZ = 16
NY = 4
SHARDS = NZ * NY
BLOCK = 6
SLOTS = SHARDS * BLOCK
PACK = 320
COLS = 384
HEADS = COLS // HDIM
FAR = 7
LANES = 384
TENSOR = 8

Q, K, V, DV, DQ, DK = range(6)


def mm(a, b):
    return lax.dot_general(a, b, (((1,), (0,)), ((), ())), preferred_element_type=F32)


def mm_nt(a, b):
    return lax.dot_general(a, b, (((1,), (1,)), ((), ())), preferred_element_type=F32)


def mm_tn(a, b):
    return lax.dot_general(a, b, (((0,), (0,)), ((), ())), preferred_element_type=F32)


def iota(shape, dim):
    return lax.broadcasted_iota(I32, shape, dim)


def sixth(x):
    return (x * 10923) >> 16


def one_hot(row, rows):
    return jnp.where(iota((rows, row.shape[1]), 0) == row, 1.0, 0.0).astype(BF)


def row_sums(product):
    high = product.astype(BF)
    low = (product - high.astype(F32)).astype(BF)
    ones = jnp.ones((8, COLS), BF)
    return mm_nt(ones, high) + mm_nt(ones, low)


def column(row):
    return jnp.transpose(jnp.broadcast_to(row, (128, LANES)))[:PACK, 0:1]


def kernel(
    kept_hbm, dest_hbm, offset_hbm, image_hbm, q_hbm, k_hbm, v_hbm, g_hbm,
    att_hbm, dq_hbm, dk_hbm, dv_hbm,
    kept_ref, dest_ref, offset_ref, image_ref, qkv, cot, attended, home, ysend, yrecv, zsend, zrecv, xsend, xrecv,
    gather_y, unpack, unpack_y, place, place_y, back, back_y, regroup, regroup_inv,
    probs, tanhs, packed_q, packed_k, normed_q, normed_k, grad_q, grad_k,
    far_sem, load_sem, store_sem, ysend_sem, yrecv_sem, zsend_sem, zrecv_sem, xsend_sem, xrecv_sem,
):
    dp = lax.axis_index("dp")
    tensor = lax.axis_index("tensor")
    z, y = dp // NY, dp % NY

    def y_peer(i):
        return lax.rem(y + i + 1, NY)

    def z_peer(i):
        half = NZ // 2 - (i + 1) // 2
        return lax.rem(z + jnp.where(i % 2 == 0, half, NZ - half), NZ)

    def x_peer(i):
        return lax.rem(tensor + i + 1, TENSOR)

    loads = [
        pltpu.make_async_copy(source, target, load_sem.at[i])
        for i, (source, target) in enumerate(
            (
                (kept_hbm, kept_ref), (dest_hbm, dest_ref), (offset_hbm, offset_ref),
                (image_hbm, image_ref), (q_hbm, qkv.at[0]), (k_hbm, qkv.at[1]),
                (v_hbm, qkv.at[2]), (g_hbm, cot),
            )
        )
    ]
    for load in loads:
        load.start()
    barrier = pltpu.get_barrier_semaphore()

    def greet_z(i, carry):
        pl.semaphore_signal(
            barrier, inc=1, device_id={"dp": z_peer(i) * NY + y}, device_id_type=MESH
        )
        return carry

    def greet_y(i, carry):
        pl.semaphore_signal(
            barrier, inc=1, device_id={"dp": z * NY + y_peer(i)}, device_id_type=MESH
        )
        return carry

    def greet_x(i, carry):
        pl.semaphore_signal(barrier, inc=1, device_id={"tensor": x_peer(i)}, device_id_type=MESH)
        return carry

    lax.fori_loop(FAR, NZ - 1, greet_z, 0)
    lax.fori_loop(0, NY - 1, greet_y, 0)
    lax.fori_loop(0, TENSOR - 1, greet_x, 0)

    stores = [
        pltpu.make_async_copy(source, target, store_sem.at[i])
        for i, (source, target) in enumerate(
            ((attended, att_hbm), (home.at[0], dv_hbm), (home.at[1], dq_hbm), (home.at[2], dk_hbm))
        )
    ]

    def send_y(array):
        def one(i, carry):
            peer = y_peer(i)
            pltpu.make_async_remote_copy(
                ysend.at[array, peer], yrecv.at[array, y], ysend_sem.at[array], yrecv_sem.at[array],
                device_id={"dp": z * NY + peer}, device_id_type=MESH,
            ).start()
            return carry

        lax.fori_loop(0, NY - 1, one, 0)
        yrecv[array, y] = ysend[array, y]

    def wait_y(array):
        part = yrecv.at[array, pl.ds(0, NY - 1)]
        pltpu.make_async_copy(part, part, yrecv_sem.at[array]).wait()
        return yrecv[array].reshape(SLOTS, COLS)

    def send_z(array, first=0, last=NZ - 1):
        def one(i, carry):
            peer = z_peer(i)
            pltpu.make_async_remote_copy(
                zsend.at[array, peer], zrecv.at[array, z], zsend_sem.at[array], zrecv_sem.at[array],
                device_id={"dp": peer * NY + y}, device_id_type=MESH,
            ).start()
            return carry

        lax.fori_loop(first, last, one, 0)
        if first == 0:
            zrecv[array, z] = zsend[array, z]

    def wait_z(array):
        part = zrecv.at[array, pl.ds(0, NZ - 1)]
        pltpu.make_async_copy(part, part, zrecv_sem.at[array]).wait()
        return zrecv[array].reshape(SLOTS, COLS)

    def send_x(which):
        def one(i, carry):
            peer = x_peer(i)
            pltpu.make_async_remote_copy(
                xsend.at[which], xrecv.at[which, tensor], xsend_sem.at[which], xrecv_sem.at[which],
                device_id={"tensor": peer}, device_id_type=MESH,
            ).start()
            return carry

        lax.fori_loop(0, TENSOR - 1, one, 0)
        xrecv[which, tensor] = xsend[which]

    def wait_x(which):
        part = xrecv.at[which, pl.ds(0, TENSOR - 1)]
        pltpu.make_async_copy(part, part, xrecv_sem.at[which]).wait()
        return jnp.sum(xrecv[which], axis=0)

    def put_y(array, rows):
        ysend[array] = rows.astype(BF).reshape(NY, SLOTS // NY, COLS)

    def put_z(array, rows):
        zsend[array] = rows.astype(BF).reshape(NZ, SLOTS // NZ, COLS)

    line = iota((1, SLOTS), 1)
    unit = sixth(line)
    spot = line - BLOCK * unit
    unit_y = (unit & (NZ - 1)) * NY + (unit >> 4)
    down = iota((SLOTS, SLOTS), 0)
    across = iota((SLOTS, SLOTS), 1)
    earlier = jnp.where((sixth(down) == sixth(across)) & (down < across), 1.0, 0.0).astype(BF)
    for load in loads[:4]:
        load.wait()
    kept = kept_ref[...].reshape(1, SLOTS)
    before = mm(jnp.broadcast_to(kept.astype(F32), (8, SLOTS)).astype(BF), earlier)[0:1]
    before = before.astype(I32)
    which = iota((8, SHARDS), 0)
    dest = dest_ref[...].reshape(1, SHARDS)
    offset = offset_ref[...].reshape(1, SHARDS)
    parts = jnp.where(which == 0, dest, jnp.where(which == 1, offset >> 4, offset & 15))
    parts = parts.astype(F32).astype(BF)
    spread = mm(parts, one_hot(unit, SHARDS)).astype(I32)
    spread_y = mm(parts, one_hot(unit_y, SHARDS)).astype(I32)
    dest_slot = spread[0:1]
    first = spread[1:2] * 16 + spread[2:3]
    first_y = spread_y[1:2] * 16 + spread_y[2:3]
    dest_y = (dest_slot & (NY - 1)) * NZ + (dest_slot >> 2)
    target = jnp.where(kept == 1, dest_slot * BLOCK + before, -1)
    target_y = jnp.where(kept == 1, dest_y * BLOCK + before, -1)

    gather = one_hot(target, SLOTS)
    loads[4].wait()
    put_z(Q, mm(gather, qkv[0]))
    pl.semaphore_wait(barrier, (NZ - 1 - FAR) + (NY - 1) + (TENSOR - 1))

    def pass_on(i, carry):
        pl.semaphore_signal(
            far_sem, inc=1, device_id={"dp": z_peer(i) * NY + y}, device_id_type=MESH
        )
        return carry

    lax.fori_loop(FAR, FAR + 2, pass_on, 0)
    send_z(Q, FAR, NZ - 1)

    gather_y[...] = one_hot(target_y, SLOTS)
    loads[5].wait()
    put_y(K, mm(gather_y[...], qkv[1]))
    send_y(K)
    loads[6].wait()
    put_y(V, mm(gather_y[...], qkv[2]))
    send_y(V)

    pl.semaphore_wait(far_sem, 2)
    send_z(Q, 0, FAR)

    identity = jnp.where(down == across, 1.0, 0.0).astype(BF)
    regroup[...] = one_hot(unit_y * BLOCK + spot, SLOTS)
    unpack[...] = mm_nt(identity, gather).astype(BF)
    place[...] = one_hot(first + spot, PACK)
    place_y[...] = one_hot(first_y + spot, PACK)
    back[...] = mm_nt(identity, place[...]).astype(BF)
    back_y[...] = mm_nt(identity, place_y[...]).astype(BF)
    unpack_y[...] = mm_nt(identity, gather_y[...]).astype(BF)
    unit_n = (unit & (NY - 1)) * NZ + (unit >> 2)
    regroup_inv[...] = one_hot(unit_n * BLOCK + spot, SLOTS)

    image = jnp.broadcast_to(image_ref[...].reshape(1, PACK), (8, PACK))
    image_hot = jnp.where(image == iota((8, PACK), 0), 1.0, 0.0).astype(BF)
    same = mm_tn(image_hot, image_hot)

    xsend[...] = jnp.zeros((3, 8, LANES), F32)

    put_z(K, mm(regroup[...], wait_y(K)))
    put_z(V, mm(regroup[...], wait_y(V)))
    send_z(K)

    put_y(Q, mm(regroup_inv[...], wait_z(Q)))
    send_y(Q)
    packed = mm(place_y[...], wait_y(Q))
    packed_q[...] = packed
    xsend[0, :, :PACK] = row_sums(packed * packed)
    send_x(0)
    send_z(V)

    packed = mm(place[...], wait_z(K))
    packed_k[...] = packed
    xsend[1, :, :PACK] = row_sums(packed * packed)
    send_x(1)

    scale_q = column(lax.rsqrt(wait_x(0)[0:1] / WIDTH + EPSILON))
    packed_q[...] = packed_q[...] * scale_q
    normed_q[...] = packed_q[...].astype(BF)
    scale_k = column(lax.rsqrt(wait_x(1)[0:1] / WIDTH + EPSILON))
    packed_k[...] = packed_k[...] * scale_k
    normed_k[...] = packed_k[...].astype(BF)

    loads[7].wait()
    value_back = []
    for h in range(HEADS):
        cols = slice(h * HDIM, (h + 1) * HDIM)
        raw = mm_nt(normed_q[:, cols], normed_k[:, cols]) / math.sqrt(HDIM)
        bent = jnp.tanh(raw / SOFT_LIMIT)
        weight = jnp.exp(SOFT_LIMIT * bent) * same
        prob = weight * (1.0 / jnp.sum(weight, axis=1, keepdims=True))
        probs[h] = prob
        tanhs[h] = bent
        value_back.append(mm_tn(prob.astype(BF), cot[:, cols]).astype(BF))
    put_z(DV, mm(back[...], jnp.concatenate(value_back, axis=1)))
    send_z(DV)

    value = mm(place[...], wait_z(V)).astype(BF)
    for h in range(HEADS):
        cols = slice(h * HDIM, (h + 1) * HDIM)
        prob = probs[h]
        bent = tanhs[h]
        prob_grad = mm_nt(cot[:, cols], value[:, cols])
        inner = jnp.sum(prob * prob_grad, axis=1, keepdims=True)
        score = prob * (prob_grad - inner) * (1.0 - bent * bent) / math.sqrt(HDIM)
        score = score.astype(BF)
        grad_q[:, cols] = mm(score, normed_k[:, cols])
        grad_k[:, cols] = mm_tn(score, normed_q[:, cols])
    sums_q = row_sums(grad_q[...] * packed_q[...])
    sums_k = row_sums(grad_k[...] * packed_k[...])
    xsend[2, :, :PACK] = jnp.where(iota((8, PACK), 0) == 0, sums_q, sums_k)
    send_x(2)
    for h in range(HEADS):
        cols = slice(h * HDIM, (h + 1) * HDIM)
        attended[:, cols] = mm(probs[h].astype(BF), value[:, cols]).astype(BF)
    stores[0].start()
    inner = wait_x(2) / WIDTH
    grad = scale_q * (grad_q[...] - packed_q[...] * column(inner[0:1]))
    put_z(DQ, mm(back[...], grad.astype(BF)))
    grad = scale_k * (grad_k[...] - packed_k[...] * column(inner[1:2]))
    put_y(DK, mm(back_y[...], grad.astype(BF)))
    send_z(DQ)
    send_y(DK)
    put_z(DK, mm(regroup[...], wait_y(DK)))
    put_y(DV, mm(regroup_inv[...], wait_z(DV)))
    send_y(DV)
    send_z(DK)
    home[0] = mm(unpack_y[...], wait_y(DV)).astype(BF)
    stores[1].start()
    put_y(DQ, mm(regroup_inv[...], wait_z(DQ)))
    send_y(DQ)
    home[1] = mm(unpack_y[...], wait_y(DQ)).astype(BF)
    stores[2].start()
    home[2] = mm(unpack[...], wait_z(DK)).astype(BF)
    stores[3].start()

    for array in range(6):
        part = ysend.at[array, pl.ds(0, NY - 1)]
        pltpu.make_async_copy(part, part, ysend_sem.at[array]).wait()
        part = zsend.at[array, pl.ds(0, NZ - 1)]
        pltpu.make_async_copy(part, part, zsend_sem.at[array]).wait()
    for which in range(3):
        part = xrecv.at[which, pl.ds(0, TENSOR - 1)]
        pltpu.make_async_copy(part, part, xsend_sem.at[which]).wait()
    for copy in stores:
        copy.wait()


def store(*refs):
    for source, target in zip(refs[:4], refs[4:]):
        target[...] = source[...]


def local(
    query_rows, key_rows, value_rows, kept_mask, block_dest, pack_offset, pack_image, grad_attended
):
    hbm = pl.BlockSpec(memory_space=pltpu.HBM)
    vmem = pl.BlockSpec(memory_space=pltpu.VMEM)
    dma = pltpu.SemaphoreType.DMA
    slots = jax.ShapeDtypeStruct((SLOTS, COLS), BF)
    square = pltpu.VMEM((SLOTS, SLOTS), BF)
    results = pl.pallas_call(
        kernel,
        out_shape=(jax.ShapeDtypeStruct((PACK, COLS), BF), slots, slots, slots),
        in_specs=[hbm] * 8,
        out_specs=(hbm,) * 4,
        scratch_shapes=[
            pltpu.VMEM((SLOTS,), I32),
            pltpu.VMEM((SHARDS,), I32),
            pltpu.VMEM((SHARDS,), I32),
            pltpu.VMEM((PACK,), I32),
            pltpu.VMEM((3, SLOTS, COLS), BF),
            pltpu.VMEM((PACK, COLS), BF),
            pltpu.VMEM((PACK, COLS), BF),
            pltpu.VMEM((3, SLOTS, COLS), BF),
            pltpu.VMEM((6, NY, SLOTS // NY, COLS), BF),
            pltpu.VMEM((6, NY, SLOTS // NY, COLS), BF),
            pltpu.VMEM((6, NZ, SLOTS // NZ, COLS), BF),
            pltpu.VMEM((6, NZ, SLOTS // NZ, COLS), BF),
            pltpu.VMEM((3, 8, LANES), F32),
            pltpu.VMEM((3, TENSOR, 8, LANES), F32),
            square,
            square,
            square,
            pltpu.VMEM((PACK, SLOTS), BF),
            pltpu.VMEM((PACK, SLOTS), BF),
            pltpu.VMEM((SLOTS, PACK), BF),
            pltpu.VMEM((SLOTS, PACK), BF),
            square,
            square,
            pltpu.VMEM((HEADS, PACK, PACK), F32),
            pltpu.VMEM((HEADS, PACK, PACK), F32),
            pltpu.VMEM((PACK, COLS), F32),
            pltpu.VMEM((PACK, COLS), F32),
            pltpu.VMEM((PACK, COLS), BF),
            pltpu.VMEM((PACK, COLS), BF),
            pltpu.VMEM((PACK, COLS), F32),
            pltpu.VMEM((PACK, COLS), F32),
            pltpu.SemaphoreType.REGULAR,
            dma((8,)),
            dma((4,)),
            dma((6,)),
            dma((6,)),
            dma((6,)),
            dma((6,)),
            dma((3,)),
            dma((3,)),
        ],
        compiler_params=pltpu.CompilerParams(
            collective_id=0, has_side_effects=True, vmem_limit_bytes=62 * 2**20
        ),
        cost_estimate=pl.CostEstimate(
            flops=4 * 10**9, bytes_accessed=3 * 10**6, transcendentals=10**6
        ),
        name="repack_attention",
    )(
        kept_mask,
        block_dest,
        pack_offset,
        pack_image,
        query_rows,
        key_rows,
        value_rows,
        grad_attended,
    )
    return pl.pallas_call(
        store,
        out_shape=(jax.ShapeDtypeStruct((PACK, COLS), BF), slots, slots, slots),
        in_specs=[vmem] * 4,
        out_specs=(vmem,) * 4,
        compiler_params=pltpu.CompilerParams(vmem_limit_bytes=62 * 2**20),
        name="store_outputs",
    )(*results)


def solution(mesh):
    in_specs = (
        P("dp", "tensor"),
        P("dp", "tensor"),
        P("dp", "tensor"),
        P("dp"),
        P("dp"),
        P("dp"),
        P("dp"),
        P("dp", "tensor"),
    )
    out_specs = (P("dp", "tensor"), P("dp", "tensor"), P("dp", "tensor"), P("dp", "tensor"))
    return jax.shard_map(local, mesh=mesh, in_specs=in_specs, out_specs=out_specs, check_vma=False)
```

```python
import math

import jax
import jax.numpy as jnp
from jax import lax
from jax.experimental import pallas as pl
from jax.experimental.pallas import tpu as pltpu
from jax.sharding import PartitionSpec as P

HDIM = 128
WIDTH = 3072
SOFT_LIMIT = 20.0
EPSILON = 1e-06

MESH = pl.DeviceIdType.MESH
BF = jnp.bfloat16
F32 = jnp.float32
I32 = jnp.int32

NZ = 16
NY = 4
SHARDS = NZ * NY
BLOCK = 6
SLOTS = SHARDS * BLOCK
PACK = 320
COLS = 384
HEADS = COLS // HDIM
FAR = 7
LANES = 384
TENSOR = 8

Q, K, V, DV, DQ, DK = range(6)


def mm(a, b):
    return lax.dot_general(a, b, (((1,), (0,)), ((), ())), preferred_element_type=F32)


def mm_nt(a, b):
    return lax.dot_general(a, b, (((1,), (1,)), ((), ())), preferred_element_type=F32)


def mm_tn(a, b):
    return lax.dot_general(a, b, (((0,), (0,)), ((), ())), preferred_element_type=F32)


def iota(shape, dim):
    return lax.broadcasted_iota(I32, shape, dim)


def sixth(x):
    return (x * 10923) >> 16


def one_hot(row, rows):
    return jnp.where(iota((rows, row.shape[1]), 0) == row, 1.0, 0.0).astype(BF)


def row_sums(product):
    high = product.astype(BF)
    low = (product - high.astype(F32)).astype(BF)
    ones = jnp.ones((8, COLS), BF)
    return mm_nt(ones, high) + mm_nt(ones, low)


def column(row):
    return jnp.transpose(jnp.broadcast_to(row, (128, LANES)))[:PACK, 0:1]


def kernel(
    kept_hbm, dest_hbm, offset_hbm, image_hbm, q_hbm, k_hbm, v_hbm, g_hbm,
    att_hbm, dq_hbm, dv_hbm, last_hbm, unpack_hbm,
    kept_ref, dest_ref, offset_ref, image_ref, qkv, cot, attended, home, ysend, yrecv, zsend, zrecv, xsend, xrecv,
    gather_y, unpack, unpack_y, place, place_y, back, back_y, regroup, regroup_inv,
    probs, tanhs, scores, packed_q, packed_k, normed_q, normed_k, grad_q, grad_k,
    far_sem, own_sem, load_sem, store_sem, ysend_sem, yrecv_sem, zsend_sem, zrecv_sem, xsend_sem, xrecv_sem,
):
    dp = lax.axis_index("dp")
    tensor = lax.axis_index("tensor")
    z, y = dp // NY, dp % NY

    def y_peer(i):
        return lax.rem(y + i + 1, NY)

    def z_peer(i):
        half = NZ // 2 - (i + 1) // 2
        return lax.rem(z + jnp.where(i % 2 == 0, half, NZ - half), NZ)

    def x_peer(i):
        return lax.rem(tensor + i + 1, TENSOR)

    loads = [
        pltpu.make_async_copy(source, target, load_sem.at[i])
        for i, (source, target) in enumerate(
            (
                (kept_hbm, kept_ref), (dest_hbm, dest_ref), (offset_hbm, offset_ref),
                (image_hbm, image_ref), (q_hbm, qkv.at[0]), (k_hbm, qkv.at[1]),
                (v_hbm, qkv.at[2]), (g_hbm, cot),
            )
        )
    ]
    for load in loads:
        load.start()
    barrier = pltpu.get_barrier_semaphore()

    def greet_z(i, carry):
        pl.semaphore_signal(
            barrier, inc=1, device_id={"dp": z_peer(i) * NY + y}, device_id_type=MESH
        )
        return carry

    def greet_y(i, carry):
        pl.semaphore_signal(
            barrier, inc=1, device_id={"dp": z * NY + y_peer(i)}, device_id_type=MESH
        )
        return carry

    def greet_x(i, carry):
        pl.semaphore_signal(barrier, inc=1, device_id={"tensor": x_peer(i)}, device_id_type=MESH)
        return carry

    lax.fori_loop(FAR, NZ - 1, greet_z, 0)
    lax.fori_loop(0, NY - 1, greet_y, 0)
    lax.fori_loop(0, TENSOR - 1, greet_x, 0)

    own_last = pltpu.make_async_copy(zsend.at[DK, z], last_hbm.at[z], own_sem)
    stores = [
        pltpu.make_async_copy(source, target, store_sem.at[i])
        for i, (source, target) in enumerate(
            ((attended, att_hbm), (home.at[0], dv_hbm), (home.at[1], dq_hbm), (unpack, unpack_hbm))
        )
    ]

    def send_y(array):
        def one(i, carry):
            peer = y_peer(i)
            pltpu.make_async_remote_copy(
                ysend.at[array, peer], yrecv.at[array, y], ysend_sem.at[array], yrecv_sem.at[array],
                device_id={"dp": z * NY + peer}, device_id_type=MESH,
            ).start()
            return carry

        lax.fori_loop(0, NY - 1, one, 0)
        yrecv[array, y] = ysend[array, y]

    def wait_y(array):
        part = yrecv.at[array, pl.ds(0, NY - 1)]
        pltpu.make_async_copy(part, part, yrecv_sem.at[array]).wait()
        return yrecv[array].reshape(SLOTS, COLS)

    def send_z(array, first=0, last=NZ - 1):
        target = last_hbm if array == DK else zrecv.at[array]

        def one(i, carry):
            peer = z_peer(i)
            pltpu.make_async_remote_copy(
                zsend.at[array, peer], target.at[z], zsend_sem.at[array], zrecv_sem.at[array],
                device_id={"dp": peer * NY + y}, device_id_type=MESH,
            ).start()
            return carry

        lax.fori_loop(first, last, one, 0)
        if array == DK:
            own_last.start()
        elif first == 0:
            zrecv[array, z] = zsend[array, z]

    def wait_z(array):
        part = zrecv.at[array, pl.ds(0, NZ - 1)]
        pltpu.make_async_copy(part, part, zrecv_sem.at[array]).wait()
        return zrecv[array].reshape(SLOTS, COLS)

    def send_x(which):
        def one(i, carry):
            peer = x_peer(i)
            pltpu.make_async_remote_copy(
                xsend.at[which], xrecv.at[which, tensor], xsend_sem.at[which], xrecv_sem.at[which],
                device_id={"tensor": peer}, device_id_type=MESH,
            ).start()
            return carry

        lax.fori_loop(0, TENSOR - 1, one, 0)
        xrecv[which, tensor] = xsend[which]

    def wait_x(which):
        part = xrecv.at[which, pl.ds(0, TENSOR - 1)]
        pltpu.make_async_copy(part, part, xrecv_sem.at[which]).wait()
        return jnp.sum(xrecv[which], axis=0)

    def put_y(array, rows):
        ysend[array] = rows.astype(BF).reshape(NY, SLOTS // NY, COLS)

    def put_z(array, rows):
        zsend[array] = rows.astype(BF).reshape(NZ, SLOTS // NZ, COLS)

    line = iota((1, SLOTS), 1)
    unit = sixth(line)
    spot = line - BLOCK * unit
    unit_y = (unit & (NZ - 1)) * NY + (unit >> 4)
    down = iota((SLOTS, SLOTS), 0)
    across = iota((SLOTS, SLOTS), 1)
    earlier = jnp.where((sixth(down) == sixth(across)) & (down < across), 1.0, 0.0).astype(BF)
    for load in loads[:4]:
        load.wait()
    kept = kept_ref[...].reshape(1, SLOTS)
    before = mm(jnp.broadcast_to(kept.astype(F32), (8, SLOTS)).astype(BF), earlier)[0:1]
    before = before.astype(I32)
    which = iota((8, SHARDS), 0)
    dest = dest_ref[...].reshape(1, SHARDS)
    offset = offset_ref[...].reshape(1, SHARDS)
    parts = jnp.where(which == 0, dest, jnp.where(which == 1, offset >> 4, offset & 15))
    parts = parts.astype(F32).astype(BF)
    spread = mm(parts, one_hot(unit, SHARDS)).astype(I32)
    dest_slot = spread[0:1]
    target = jnp.where(kept == 1, dest_slot * BLOCK + before, -1)

    gather = one_hot(target, SLOTS)
    loads[4].wait()
    put_z(Q, mm(gather, qkv[0]))
    pl.semaphore_wait(barrier, (NZ - 1 - FAR) + (NY - 1) + (TENSOR - 1))

    def pass_on(i, carry):
        pl.semaphore_signal(
            far_sem, inc=1, device_id={"dp": z_peer(i) * NY + y}, device_id_type=MESH
        )
        return carry

    lax.fori_loop(FAR, FAR + 2, pass_on, 0)
    send_z(Q, FAR, NZ - 1)

    dest_y = (dest_slot & (NY - 1)) * NZ + (dest_slot >> 2)
    gather_y[...] = one_hot(jnp.where(kept == 1, dest_y * BLOCK + before, -1), SLOTS)
    loads[5].wait()
    put_y(K, mm(gather_y[...], qkv[1]))
    send_y(K)
    loads[6].wait()
    put_y(V, mm(gather_y[...], qkv[2]))
    send_y(V)

    pl.semaphore_wait(far_sem, 2)
    send_z(Q, 0, FAR)

    identity = jnp.where(down == across, 1.0, 0.0).astype(BF)
    regroup[...] = one_hot(unit_y * BLOCK + spot, SLOTS)
    unpack[...] = mm_nt(identity, gather).astype(BF)
    stores[3].start()
    spread_y = mm(parts, one_hot(unit_y, SHARDS)).astype(I32)
    first = spread[1:2] * 16 + spread[2:3]
    first_y = spread_y[1:2] * 16 + spread_y[2:3]
    place[...] = one_hot(first + spot, PACK)
    place_y[...] = one_hot(first_y + spot, PACK)
    back[...] = mm_nt(identity, place[...]).astype(BF)
    back_y[...] = mm_nt(identity, place_y[...]).astype(BF)
    unpack_y[...] = mm_nt(identity, gather_y[...]).astype(BF)
    unit_n = (unit & (NY - 1)) * NZ + (unit >> 2)
    regroup_inv[...] = one_hot(unit_n * BLOCK + spot, SLOTS)

    image = jnp.broadcast_to(image_ref[...].reshape(1, PACK), (8, PACK))
    image_hot = jnp.where(image == iota((8, PACK), 0), 1.0, 0.0).astype(BF)
    same = mm_tn(image_hot, image_hot)

    xsend[...] = jnp.zeros((4, 8, LANES), F32)

    put_z(K, mm(regroup[...], wait_y(K)))
    put_z(V, mm(regroup[...], wait_y(V)))
    send_z(K)

    put_y(Q, mm(regroup_inv[...], wait_z(Q)))
    send_y(Q)
    packed = mm(place_y[...], wait_y(Q))
    packed_q[...] = packed
    xsend[0, :, :PACK] = row_sums(packed * packed)
    send_x(0)
    send_z(V)

    packed = mm(place[...], wait_z(K))
    packed_k[...] = packed
    xsend[1, :, :PACK] = row_sums(packed * packed)
    send_x(1)

    scale_q = column(lax.rsqrt(wait_x(0)[0:1] / WIDTH + EPSILON))
    packed_q[...] = packed_q[...] * scale_q
    normed_q[...] = packed_q[...].astype(BF)
    scale_k = column(lax.rsqrt(wait_x(1)[0:1] / WIDTH + EPSILON))
    packed_k[...] = packed_k[...] * scale_k
    normed_k[...] = packed_k[...].astype(BF)

    loads[7].wait()
    value_back = []
    for h in range(HEADS):
        cols = slice(h * HDIM, (h + 1) * HDIM)
        raw = mm_nt(normed_q[:, cols], normed_k[:, cols]) / math.sqrt(HDIM)
        bent = jnp.tanh(raw / SOFT_LIMIT)
        weight = jnp.exp(SOFT_LIMIT * bent) * same
        prob = weight * (1.0 / jnp.sum(weight, axis=1, keepdims=True))
        probs[h] = prob
        tanhs[h] = bent
        value_back.append(mm_tn(prob.astype(BF), cot[:, cols]).astype(BF))
    put_z(DV, mm(back[...], jnp.concatenate(value_back, axis=1)))
    send_z(DV)

    value = mm(place[...], wait_z(V)).astype(BF)
    for h in range(HEADS):
        cols = slice(h * HDIM, (h + 1) * HDIM)
        prob = probs[h]
        bent = tanhs[h]
        prob_grad = mm_nt(cot[:, cols], value[:, cols])
        inner = jnp.sum(prob * prob_grad, axis=1, keepdims=True)
        score = prob * (prob_grad - inner) * (1.0 - bent * bent) / math.sqrt(HDIM)
        scores[h] = score.astype(BF)
        grad_q[:, cols] = mm(scores[h], normed_k[:, cols])
    xsend[2, :, :PACK] = row_sums(grad_q[...] * packed_q[...])
    send_x(2)
    for h in range(HEADS):
        cols = slice(h * HDIM, (h + 1) * HDIM)
        grad_k[:, cols] = mm_tn(scores[h], normed_q[:, cols])
    xsend[3, :, :PACK] = row_sums(grad_k[...] * packed_k[...])
    send_x(3)
    for h in range(HEADS):
        cols = slice(h * HDIM, (h + 1) * HDIM)
        attended[:, cols] = mm(probs[h].astype(BF), value[:, cols]).astype(BF)
    stores[0].start()
    inner = column(wait_x(2)[0:1] / WIDTH)
    grad = scale_q * (grad_q[...] - packed_q[...] * inner)
    put_z(DQ, mm(back[...], grad.astype(BF)))
    send_z(DQ)
    inner = column(wait_x(3)[0:1] / WIDTH)
    grad = scale_k * (grad_k[...] - packed_k[...] * inner)
    put_y(DK, mm(back_y[...], grad.astype(BF)))
    send_y(DK)
    put_z(DK, mm(regroup[...], wait_y(DK)))
    put_y(DV, mm(regroup_inv[...], wait_z(DV)))
    send_y(DV)
    send_z(DK)
    home[0] = mm(unpack_y[...], wait_y(DV)).astype(BF)
    stores[1].start()
    put_y(DQ, mm(regroup_inv[...], wait_z(DQ)))
    send_y(DQ)
    home[1] = mm(unpack_y[...], wait_y(DQ)).astype(BF)
    stores[2].start()
    part = last_hbm.at[pl.ds(0, NZ - 1)]
    pltpu.make_async_copy(part, part, zrecv_sem.at[DK]).wait()
    own_last.wait()

    for array in range(6):
        part = ysend.at[array, pl.ds(0, NY - 1)]
        pltpu.make_async_copy(part, part, ysend_sem.at[array]).wait()
        part = zsend.at[array, pl.ds(0, NZ - 1)]
        pltpu.make_async_copy(part, part, zsend_sem.at[array]).wait()
    for which in range(4):
        part = xrecv.at[which, pl.ds(0, TENSOR - 1)]
        pltpu.make_async_copy(part, part, xsend_sem.at[which]).wait()
    for copy in stores:
        copy.wait()


def finish(
    att_in, dq_in, dv_in, last_in, unpack_in, att_out, dq_out, dk_out, dv_out,
    att, dq, dv, last, unpack, dk, load_sem, store_sem,
):
    loads = [
        pltpu.make_async_copy(source, target, load_sem.at[i])
        for i, (source, target) in enumerate(
            ((last_in, last), (unpack_in, unpack), (att_in, att), (dq_in, dq), (dv_in, dv))
        )
    ]
    stores = [
        pltpu.make_async_copy(source, target, store_sem.at[i])
        for i, (source, target) in enumerate(
            ((att, att_out), (dq, dq_out), (dv, dv_out), (dk, dk_out))
        )
    ]
    for load in loads:
        load.start()
    loads[0].wait()
    loads[1].wait()
    dk[...] = mm(unpack[...], last[...].reshape(SLOTS, COLS)).astype(BF)
    stores[3].start()
    for i in range(3):
        loads[i + 2].wait()
        stores[i].start()
    for copy in stores:
        copy.wait()


def local(
    query_rows, key_rows, value_rows, kept_mask, block_dest, pack_offset, pack_image, grad_attended
):
    hbm = pl.BlockSpec(memory_space=pltpu.HBM)
    dma = pltpu.SemaphoreType.DMA
    slots = jax.ShapeDtypeStruct((SLOTS, COLS), BF)
    square = pltpu.VMEM((SLOTS, SLOTS), BF)
    results = pl.pallas_call(
        kernel,
        out_shape=(
            jax.ShapeDtypeStruct((PACK, COLS), BF),
            slots,
            slots,
            jax.ShapeDtypeStruct((NZ, SLOTS // NZ, COLS), BF),
            jax.ShapeDtypeStruct((SLOTS, SLOTS), BF),
        ),
        in_specs=[hbm] * 8,
        out_specs=(hbm,) * 5,
        scratch_shapes=[
            pltpu.VMEM((SLOTS,), I32),
            pltpu.VMEM((SHARDS,), I32),
            pltpu.VMEM((SHARDS,), I32),
            pltpu.VMEM((PACK,), I32),
            pltpu.VMEM((3, SLOTS, COLS), BF),
            pltpu.VMEM((PACK, COLS), BF),
            pltpu.VMEM((PACK, COLS), BF),
            pltpu.VMEM((3, SLOTS, COLS), BF),
            pltpu.VMEM((6, NY, SLOTS // NY, COLS), BF),
            pltpu.VMEM((6, NY, SLOTS // NY, COLS), BF),
            pltpu.VMEM((6, NZ, SLOTS // NZ, COLS), BF),
            pltpu.VMEM((6, NZ, SLOTS // NZ, COLS), BF),
            pltpu.VMEM((4, 8, LANES), F32),
            pltpu.VMEM((4, TENSOR, 8, LANES), F32),
            square,
            square,
            square,
            pltpu.VMEM((PACK, SLOTS), BF),
            pltpu.VMEM((PACK, SLOTS), BF),
            pltpu.VMEM((SLOTS, PACK), BF),
            pltpu.VMEM((SLOTS, PACK), BF),
            square,
            square,
            pltpu.VMEM((HEADS, PACK, PACK), F32),
            pltpu.VMEM((HEADS, PACK, PACK), F32),
            pltpu.VMEM((HEADS, PACK, PACK), BF),
            pltpu.VMEM((PACK, COLS), F32),
            pltpu.VMEM((PACK, COLS), F32),
            pltpu.VMEM((PACK, COLS), BF),
            pltpu.VMEM((PACK, COLS), BF),
            pltpu.VMEM((PACK, COLS), F32),
            pltpu.VMEM((PACK, COLS), F32),
            pltpu.SemaphoreType.REGULAR,
            dma,
            dma((8,)),
            dma((4,)),
            dma((6,)),
            dma((6,)),
            dma((6,)),
            dma((6,)),
            dma((4,)),
            dma((4,)),
        ],
        compiler_params=pltpu.CompilerParams(
            collective_id=0, has_side_effects=True, vmem_limit_bytes=62 * 2**20
        ),
        cost_estimate=pl.CostEstimate(
            flops=4 * 10**9, bytes_accessed=3 * 10**6, transcendentals=10**6
        ),
        name="repack_attention",
    )(
        kept_mask,
        block_dest,
        pack_offset,
        pack_image,
        query_rows,
        key_rows,
        value_rows,
        grad_attended,
    )
    return pl.pallas_call(
        finish,
        out_shape=(jax.ShapeDtypeStruct((PACK, COLS), BF), slots, slots, slots),
        in_specs=[hbm] * 5,
        out_specs=(hbm,) * 4,
        scratch_shapes=[
            pltpu.VMEM((PACK, COLS), BF),
            pltpu.VMEM((SLOTS, COLS), BF),
            pltpu.VMEM((SLOTS, COLS), BF),
            pltpu.VMEM((NZ, SLOTS // NZ, COLS), BF),
            pltpu.VMEM((SLOTS, SLOTS), BF),
            pltpu.VMEM((SLOTS, COLS), BF),
            dma((5,)),
            dma((4,)),
        ],
        compiler_params=pltpu.CompilerParams(vmem_limit_bytes=62 * 2**20),
        name="finish",
    )(*results)


def solution(mesh):
    in_specs = (
        P("dp", "tensor"),
        P("dp", "tensor"),
        P("dp", "tensor"),
        P("dp"),
        P("dp"),
        P("dp"),
        P("dp"),
        P("dp", "tensor"),
    )
    out_specs = (P("dp", "tensor"), P("dp", "tensor"), P("dp", "tensor"), P("dp", "tensor"))
    return jax.shard_map(local, mesh=mesh, in_specs=in_specs, out_specs=out_specs, check_vma=False)
```

```python
import math

import jax
import jax.numpy as jnp
from jax import lax
from jax.experimental import pallas as pl
from jax.experimental.pallas import tpu as pltpu
from jax.sharding import PartitionSpec as P

HDIM = 128
WIDTH = 3072
SOFT_LIMIT = 20.0
EPSILON = 1e-06

MESH = pl.DeviceIdType.MESH
BF = jnp.bfloat16
F32 = jnp.float32
I32 = jnp.int32

NZ = 16
NY = 4
SHARDS = NZ * NY
BLOCK = 6
SLOTS = SHARDS * BLOCK
PACK = 320
COLS = 384
HEADS = COLS // HDIM
FAR = 7
LANES = 384
TENSOR = 8

Q, K, V, DV, DQ, DK = range(6)


def mm(a, b):
    return lax.dot_general(a, b, (((1,), (0,)), ((), ())), preferred_element_type=F32)


def mm_nt(a, b):
    return lax.dot_general(a, b, (((1,), (1,)), ((), ())), preferred_element_type=F32)


def mm_tn(a, b):
    return lax.dot_general(a, b, (((0,), (0,)), ((), ())), preferred_element_type=F32)


def iota(shape, dim):
    return lax.broadcasted_iota(I32, shape, dim)


def sixth(x):
    return (x * 10923) >> 16


def one_hot(row, rows):
    return jnp.where(iota((rows, row.shape[1]), 0) == row, 1.0, 0.0).astype(BF)


def row_sums(product):
    high = product.astype(BF)
    low = (product - high.astype(F32)).astype(BF)
    ones = jnp.ones((8, COLS), BF)
    return mm_nt(ones, high) + mm_nt(ones, low)


def column(row):
    return jnp.transpose(jnp.broadcast_to(row, (128, LANES)))[:PACK, 0:1]


def kernel(
    kept_hbm, dest_hbm, offset_hbm, image_hbm, q_hbm, k_hbm, v_hbm, g_hbm,
    att_hbm, dq_hbm, dv_hbm, last_hbm, unpack_hbm,
    kept_ref, dest_ref, offset_ref, image_ref, qkv, cot, attended, home, ysend, yrecv, zsend, zrecv, xsend, xrecv,
    gather_y, unpack, unpack_y, place, place_y, back, back_y, regroup, regroup_inv,
    probs, tanhs, scores, packed_q, packed_k, normed_q, normed_k, grad_q, grad_k,
    far_sem, own_sem, load_sem, store_sem, ysend_sem, yrecv_sem, zsend_sem, zrecv_sem, xsend_sem, xrecv_sem,
):
    dp = lax.axis_index("dp")
    tensor = lax.axis_index("tensor")
    z, y = dp // NY, dp % NY

    def y_peer(i):
        return lax.rem(y + i + 1, NY)

    def z_peer(i):
        half = NZ // 2 - (i + 1) // 2
        return lax.rem(z + jnp.where(i % 2 == 0, half, NZ - half), NZ)

    def x_peer(i):
        return lax.rem(tensor + i + 1, TENSOR)

    loads = [
        pltpu.make_async_copy(source, target, load_sem.at[i])
        for i, (source, target) in enumerate(
            (
                (kept_hbm, kept_ref), (dest_hbm, dest_ref), (offset_hbm, offset_ref),
                (image_hbm, image_ref), (q_hbm, qkv.at[0]), (k_hbm, qkv.at[1]),
                (v_hbm, qkv.at[2]), (g_hbm, cot),
            )
        )
    ]
    for load in loads:
        load.start()
    barrier = pltpu.get_barrier_semaphore()

    def greet_z(i, carry):
        pl.semaphore_signal(
            barrier, inc=1, device_id={"dp": z_peer(i) * NY + y}, device_id_type=MESH
        )
        return carry

    def greet_y(i, carry):
        pl.semaphore_signal(
            barrier, inc=1, device_id={"dp": z * NY + y_peer(i)}, device_id_type=MESH
        )
        return carry

    def greet_x(i, carry):
        pl.semaphore_signal(barrier, inc=1, device_id={"tensor": x_peer(i)}, device_id_type=MESH)
        return carry

    lax.fori_loop(FAR, NZ - 1, greet_z, 0, unroll=True)
    lax.fori_loop(0, NY - 1, greet_y, 0, unroll=True)
    lax.fori_loop(0, TENSOR - 1, greet_x, 0, unroll=True)

    own_last = pltpu.make_async_copy(zsend.at[DK, z], last_hbm.at[z], own_sem)
    stores = [
        pltpu.make_async_copy(source, target, store_sem.at[i])
        for i, (source, target) in enumerate(
            ((attended, att_hbm), (home.at[0], dv_hbm), (home.at[1], dq_hbm), (unpack, unpack_hbm))
        )
    ]

    def send_y(array):
        def one(i, carry):
            peer = y_peer(i)
            pltpu.make_async_remote_copy(
                ysend.at[array, peer], yrecv.at[array, y], ysend_sem.at[array], yrecv_sem.at[array],
                device_id={"dp": z * NY + peer}, device_id_type=MESH,
            ).start()
            return carry

        lax.fori_loop(0, NY - 1, one, 0)
        yrecv[array, y] = ysend[array, y]

    def wait_y(array):
        part = yrecv.at[array, pl.ds(0, NY - 1)]
        pltpu.make_async_copy(part, part, yrecv_sem.at[array]).wait()
        return yrecv[array].reshape(SLOTS, COLS)

    def send_z(array, first=0, last=NZ - 1):
        target = last_hbm if array == DK else zrecv.at[array]

        def one(i, carry):
            peer = z_peer(i)
            pltpu.make_async_remote_copy(
                zsend.at[array, peer], target.at[z], zsend_sem.at[array], zrecv_sem.at[array],
                device_id={"dp": peer * NY + y}, device_id_type=MESH,
            ).start()
            return carry

        lax.fori_loop(first, last, one, 0)
        if array == DK:
            own_last.start()
        elif first == 0:
            zrecv[array, z] = zsend[array, z]

    def wait_z(array):
        part = zrecv.at[array, pl.ds(0, NZ - 1)]
        pltpu.make_async_copy(part, part, zrecv_sem.at[array]).wait()
        return zrecv[array].reshape(SLOTS, COLS)

    def send_x(which):
        def one(i, carry):
            peer = x_peer(i)
            pltpu.make_async_remote_copy(
                xsend.at[which], xrecv.at[which, tensor], xsend_sem.at[which], xrecv_sem.at[which],
                device_id={"tensor": peer}, device_id_type=MESH,
            ).start()
            return carry

        lax.fori_loop(0, TENSOR - 1, one, 0)
        xrecv[which, tensor] = xsend[which]

    def wait_x(which):
        part = xrecv.at[which, pl.ds(0, TENSOR - 1)]
        pltpu.make_async_copy(part, part, xrecv_sem.at[which]).wait()
        return jnp.sum(xrecv[which], axis=0)

    def put_y(array, rows):
        ysend[array] = rows.astype(BF).reshape(NY, SLOTS // NY, COLS)

    def put_z(array, rows):
        zsend[array] = rows.astype(BF).reshape(NZ, SLOTS // NZ, COLS)

    line = iota((1, SLOTS), 1)
    unit = sixth(line)
    spot = line - BLOCK * unit
    unit_y = (unit & (NZ - 1)) * NY + (unit >> 4)
    down = iota((SLOTS, SLOTS), 0)
    across = iota((SLOTS, SLOTS), 1)
    earlier = jnp.where((sixth(down) == sixth(across)) & (down < across), 1.0, 0.0).astype(BF)
    for load in loads[:4]:
        load.wait()
    kept = kept_ref[...].reshape(1, SLOTS)
    before = mm(jnp.broadcast_to(kept.astype(F32), (8, SLOTS)).astype(BF), earlier)[0:1]
    before = before.astype(I32)
    which = iota((8, SHARDS), 0)
    dest = dest_ref[...].reshape(1, SHARDS)
    offset = offset_ref[...].reshape(1, SHARDS)
    parts = jnp.where(which == 0, dest, jnp.where(which == 1, offset >> 4, offset & 15))
    parts = parts.astype(F32).astype(BF)
    spread = mm(parts, one_hot(unit, SHARDS)).astype(I32)
    dest_slot = spread[0:1]
    target = jnp.where(kept == 1, dest_slot * BLOCK + before, -1)

    gather = one_hot(target, SLOTS)
    loads[4].wait()
    put_z(Q, mm(gather, qkv[0]))
    pl.semaphore_wait(barrier, (NZ - 1 - FAR) + (NY - 1) + (TENSOR - 1))

    def pass_on(i, carry):
        pl.semaphore_signal(
            far_sem, inc=1, device_id={"dp": z_peer(i) * NY + y}, device_id_type=MESH
        )
        return carry

    lax.fori_loop(FAR, FAR + 2, pass_on, 0)
    send_z(Q, FAR, NZ - 1)

    dest_y = (dest_slot & (NY - 1)) * NZ + (dest_slot >> 2)
    gather_y[...] = one_hot(jnp.where(kept == 1, dest_y * BLOCK + before, -1), SLOTS)
    loads[5].wait()
    put_y(K, mm(gather_y[...], qkv[1]))
    send_y(K)
    loads[6].wait()
    put_y(V, mm(gather_y[...], qkv[2]))
    send_y(V)

    pl.semaphore_wait(far_sem, 2)
    send_z(Q, 0, FAR)

    identity = jnp.where(down == across, 1.0, 0.0).astype(BF)
    regroup[...] = one_hot(unit_y * BLOCK + spot, SLOTS)
    unpack[...] = mm_nt(identity, gather).astype(BF)
    stores[3].start()
    spread_y = mm(parts, one_hot(unit_y, SHARDS)).astype(I32)
    first = spread[1:2] * 16 + spread[2:3]
    first_y = spread_y[1:2] * 16 + spread_y[2:3]
    place[...] = one_hot(first + spot, PACK)
    place_y[...] = one_hot(first_y + spot, PACK)
    back[...] = mm_nt(identity, place[...]).astype(BF)
    back_y[...] = mm_nt(identity, place_y[...]).astype(BF)
    unpack_y[...] = mm_nt(identity, gather_y[...]).astype(BF)
    unit_n = (unit & (NY - 1)) * NZ + (unit >> 2)
    regroup_inv[...] = one_hot(unit_n * BLOCK + spot, SLOTS)

    image = jnp.broadcast_to(image_ref[...].reshape(1, PACK), (8, PACK))
    image_hot = jnp.where(image == iota((8, PACK), 0), 1.0, 0.0).astype(BF)
    same = mm_tn(image_hot, image_hot)

    xsend[...] = jnp.zeros((4, 8, LANES), F32)

    put_z(K, mm(regroup[...], wait_y(K)))
    put_z(V, mm(regroup[...], wait_y(V)))
    send_z(K)

    put_y(Q, mm(regroup_inv[...], wait_z(Q)))
    send_y(Q)
    packed = mm(place_y[...], wait_y(Q))
    packed_q[...] = packed
    xsend[0, :, :PACK] = row_sums(packed * packed)
    send_x(0)
    send_z(V)

    packed = mm(place[...], wait_z(K))
    packed_k[...] = packed
    xsend[1, :, :PACK] = row_sums(packed * packed)
    send_x(1)

    scale_q = column(lax.rsqrt(wait_x(0)[0:1] / WIDTH + EPSILON))
    packed_q[...] = packed_q[...] * scale_q
    normed_q[...] = packed_q[...].astype(BF)
    scale_k = column(lax.rsqrt(wait_x(1)[0:1] / WIDTH + EPSILON))
    packed_k[...] = packed_k[...] * scale_k
    normed_k[...] = packed_k[...].astype(BF)

    loads[7].wait()
    value_back = []
    for h in range(HEADS):
        cols = slice(h * HDIM, (h + 1) * HDIM)
        raw = mm_nt(normed_q[:, cols], normed_k[:, cols]) / math.sqrt(HDIM)
        bent = jnp.tanh(raw / SOFT_LIMIT)
        weight = jnp.exp(SOFT_LIMIT * bent) * same
        prob = weight * (1.0 / jnp.sum(weight, axis=1, keepdims=True))
        probs[h] = prob
        tanhs[h] = bent
        value_back.append(mm_tn(prob.astype(BF), cot[:, cols]).astype(BF))
    put_z(DV, mm(back[...], jnp.concatenate(value_back, axis=1)))
    send_z(DV)

    value = mm(place[...], wait_z(V)).astype(BF)
    for h in range(HEADS):
        cols = slice(h * HDIM, (h + 1) * HDIM)
        prob = probs[h]
        bent = tanhs[h]
        prob_grad = mm_nt(cot[:, cols], value[:, cols])
        inner = jnp.sum(prob * prob_grad, axis=1, keepdims=True)
        score = prob * (prob_grad - inner) * (1.0 - bent * bent) / math.sqrt(HDIM)
        scores[h] = score.astype(BF)
        grad_q[:, cols] = mm(scores[h], normed_k[:, cols])
    xsend[2, :, :PACK] = row_sums(grad_q[...] * packed_q[...])
    send_x(2)
    for h in range(HEADS):
        cols = slice(h * HDIM, (h + 1) * HDIM)
        grad_k[:, cols] = mm_tn(scores[h], normed_q[:, cols])
    xsend[3, :, :PACK] = row_sums(grad_k[...] * packed_k[...])
    send_x(3)
    for h in range(HEADS):
        cols = slice(h * HDIM, (h + 1) * HDIM)
        attended[:, cols] = mm(probs[h].astype(BF), value[:, cols]).astype(BF)
    stores[0].start()
    inner = column(wait_x(2)[0:1] / WIDTH)
    grad = scale_q * (grad_q[...] - packed_q[...] * inner)
    put_z(DQ, mm(back[...], grad.astype(BF)))
    send_z(DQ)
    inner = column(wait_x(3)[0:1] / WIDTH)
    grad = scale_k * (grad_k[...] - packed_k[...] * inner)
    put_y(DK, mm(back_y[...], grad.astype(BF)))
    send_y(DK)
    put_z(DK, mm(regroup[...], wait_y(DK)))
    put_y(DV, mm(regroup_inv[...], wait_z(DV)))
    send_y(DV)
    send_z(DK)
    home[0] = mm(unpack_y[...], wait_y(DV)).astype(BF)
    stores[1].start()
    put_y(DQ, mm(regroup_inv[...], wait_z(DQ)))
    send_y(DQ)
    home[1] = mm(unpack_y[...], wait_y(DQ)).astype(BF)
    stores[2].start()
    part = last_hbm.at[pl.ds(0, NZ - 1)]
    pltpu.make_async_copy(part, part, zrecv_sem.at[DK]).wait()
    own_last.wait()

    for array in range(6):
        part = ysend.at[array, pl.ds(0, NY - 1)]
        pltpu.make_async_copy(part, part, ysend_sem.at[array]).wait()
        part = zsend.at[array, pl.ds(0, NZ - 1)]
        pltpu.make_async_copy(part, part, zsend_sem.at[array]).wait()
    for which in range(4):
        part = xrecv.at[which, pl.ds(0, TENSOR - 1)]
        pltpu.make_async_copy(part, part, xsend_sem.at[which]).wait()
    for copy in stores:
        copy.wait()


def finish(
    att_in, dq_in, dv_in, last_in, unpack_in, att_out, dq_out, dk_out, dv_out,
    att, dq, dv, last, unpack, dk, load_sem, store_sem,
):
    loads = [
        pltpu.make_async_copy(source, target, load_sem.at[i])
        for i, (source, target) in enumerate(
            ((last_in, last), (unpack_in, unpack), (att_in, att), (dq_in, dq), (dv_in, dv))
        )
    ]
    stores = [
        pltpu.make_async_copy(source, target, store_sem.at[i])
        for i, (source, target) in enumerate(
            ((att, att_out), (dq, dq_out), (dv, dv_out), (dk, dk_out))
        )
    ]
    for load in loads:
        load.start()
    for i in range(3):
        loads[i + 2].wait()
        stores[i].start()
    loads[0].wait()
    loads[1].wait()
    dk[...] = mm(unpack[...], last[...].reshape(SLOTS, COLS)).astype(BF)
    stores[3].start()
    for copy in stores:
        copy.wait()


def local(
    query_rows, key_rows, value_rows, kept_mask, block_dest, pack_offset, pack_image, grad_attended
):
    hbm = pl.BlockSpec(memory_space=pltpu.HBM)
    dma = pltpu.SemaphoreType.DMA
    slots = jax.ShapeDtypeStruct((SLOTS, COLS), BF)
    square = pltpu.VMEM((SLOTS, SLOTS), BF)
    results = pl.pallas_call(
        kernel,
        out_shape=(
            jax.ShapeDtypeStruct((PACK, COLS), BF),
            slots,
            slots,
            jax.ShapeDtypeStruct((NZ, SLOTS // NZ, COLS), BF),
            jax.ShapeDtypeStruct((SLOTS, SLOTS), BF),
        ),
        in_specs=[hbm] * 8,
        out_specs=(hbm,) * 5,
        scratch_shapes=[
            pltpu.VMEM((SLOTS,), I32),
            pltpu.VMEM((SHARDS,), I32),
            pltpu.VMEM((SHARDS,), I32),
            pltpu.VMEM((PACK,), I32),
            pltpu.VMEM((3, SLOTS, COLS), BF),
            pltpu.VMEM((PACK, COLS), BF),
            pltpu.VMEM((PACK, COLS), BF),
            pltpu.VMEM((3, SLOTS, COLS), BF),
            pltpu.VMEM((6, NY, SLOTS // NY, COLS), BF),
            pltpu.VMEM((6, NY, SLOTS // NY, COLS), BF),
            pltpu.VMEM((6, NZ, SLOTS // NZ, COLS), BF),
            pltpu.VMEM((6, NZ, SLOTS // NZ, COLS), BF),
            pltpu.VMEM((4, 8, LANES), F32),
            pltpu.VMEM((4, TENSOR, 8, LANES), F32),
            square,
            square,
            square,
            pltpu.VMEM((PACK, SLOTS), BF),
            pltpu.VMEM((PACK, SLOTS), BF),
            pltpu.VMEM((SLOTS, PACK), BF),
            pltpu.VMEM((SLOTS, PACK), BF),
            square,
            square,
            pltpu.VMEM((HEADS, PACK, PACK), F32),
            pltpu.VMEM((HEADS, PACK, PACK), F32),
            pltpu.VMEM((HEADS, PACK, PACK), BF),
            pltpu.VMEM((PACK, COLS), F32),
            pltpu.VMEM((PACK, COLS), F32),
            pltpu.VMEM((PACK, COLS), BF),
            pltpu.VMEM((PACK, COLS), BF),
            pltpu.VMEM((PACK, COLS), F32),
            pltpu.VMEM((PACK, COLS), F32),
            pltpu.SemaphoreType.REGULAR,
            dma,
            dma((8,)),
            dma((4,)),
            dma((6,)),
            dma((6,)),
            dma((6,)),
            dma((6,)),
            dma((4,)),
            dma((4,)),
        ],
        compiler_params=pltpu.CompilerParams(
            collective_id=0, has_side_effects=True, vmem_limit_bytes=62 * 2**20
        ),
        cost_estimate=pl.CostEstimate(
            flops=4 * 10**9, bytes_accessed=3 * 10**6, transcendentals=10**6
        ),
        name="repack_attention",
    )(
        kept_mask,
        block_dest,
        pack_offset,
        pack_image,
        query_rows,
        key_rows,
        value_rows,
        grad_attended,
    )
    return pl.pallas_call(
        finish,
        out_shape=(jax.ShapeDtypeStruct((PACK, COLS), BF), slots, slots, slots),
        in_specs=[hbm] * 5,
        out_specs=(hbm,) * 4,
        scratch_shapes=[
            pltpu.VMEM((PACK, COLS), BF),
            pltpu.VMEM((SLOTS, COLS), BF),
            pltpu.VMEM((SLOTS, COLS), BF),
            pltpu.VMEM((NZ, SLOTS // NZ, COLS), BF),
            pltpu.VMEM((SLOTS, SLOTS), BF),
            pltpu.VMEM((SLOTS, COLS), BF),
            dma((5,)),
            dma((4,)),
        ],
        compiler_params=pltpu.CompilerParams(vmem_limit_bytes=62 * 2**20),
        name="finish",
    )(*results)


def solution(mesh):
    in_specs = (
        P("dp", "tensor"),
        P("dp", "tensor"),
        P("dp", "tensor"),
        P("dp"),
        P("dp"),
        P("dp"),
        P("dp"),
        P("dp", "tensor"),
    )
    out_specs = (P("dp", "tensor"), P("dp", "tensor"), P("dp", "tensor"), P("dp", "tensor"))
    return jax.shard_map(local, mesh=mesh, in_specs=in_specs, out_specs=out_specs, check_vma=False)
```
